128 devices in a mesh: depth: 8 (over x_hi, y), yband: 16 (over x_lo, z, core).
Axes of the slice: x: 4 (x_hi: 2, x_lo: 2; x = x_hi * 2 + x_lo), y: 4, z: 4, core: 2. Of those that a mesh axis runs over, the one named last changes fastest.
Arguments:
- projections: bfloat16 [16, 256, 2048], P('depth', 'yband'), may hold values from -16 to 16
- angle_index: int32 [16], replicated, may hold values from 0 to 1439
- row_ranges: int32 [16, 2], P('yband'), may hold values from -12 to 268, as said below
Outputs:
- banded: float32 [128, 128, 1024], P(('depth', 'yband'))
The draws below stay inside these ranges and needn't reach their ends.
Inputs may be any that keep to these rules, and one draw needn't show every extreme that they name: `row_ranges`: band b accepts rows from b * 16 - 12 + r to (b + 1) * 16 + 12 - q, with r and q from 0 to 11; r is 0 for the first band and q is 0 for the last.
All inputs are finite; a program needn't handle non-finite values.
Results may differ from the reference program's by a relative error of at most 0.0095.
Values may be sent and summed in bfloat16 or wider, within the bound.
A program may use at most 128 MiB of HBM per device.

```python
import math
import jax
import jax.numpy as jnp
from jax import lax

NX = 1024
NU = 2048
NANG = 1440
NP_DEV = 2
YB_DEV = 8
NPROJ = 16
NY = 128
NZ = 128
RB_DEV = 16
NV = 256
HALO = 12
BANDS = 16
N_DEPTH = 8
N_YBAND = 16


def draw_row_ranges(key, part):
    key = jax.random.fold_in(key, 11)
    low_key, high_key = jax.random.split(key)
    band_ids = jnp.arange(BANDS, dtype=jnp.int32)
    low_cut = jax.random.randint(low_key, (BANDS,), 0, HALO, dtype=jnp.int32)
    high_cut = jax.random.randint(high_key, (BANDS,), 0, HALO, dtype=jnp.int32)
    low_cut = jnp.where(band_ids == 0, 0, low_cut)
    high_cut = jnp.where(band_ids == BANDS - 1, 0, high_cut)
    row_first = band_ids * RB_DEV - HALO + low_cut
    row_last = (band_ids + 1) * RB_DEV + HALO - high_cut
    return jnp.stack([row_first, row_last], axis=1).astype(jnp.int32)


def plant(values, stream_key, smallest, largest):
    index_at = [jax.random.randint(jax.random.fold_in(stream_key, axis), (), 0, length) for axis, length in enumerate(values.shape)]
    longest = values.shape.index(max(values.shape))
    next_to = index_at[:longest] + [(index_at[longest] + 1) % values.shape[longest]] + index_at[longest + 1:]
    return values.at[tuple(index_at)].set(smallest).at[tuple(next_to)].set(largest)


def shard_levels(rng, dims, pieces, low, high):
    def one(dim, shards_of):
        steps = jax.random.uniform(jax.random.fold_in(jax.random.fold_in(rng, 6), dim), (shards_of,), jnp.float32, low / len(pieces), high / len(pieces))
        return jnp.repeat(jnp.exp(steps), dims[dim] // shards_of).reshape((-1,) + (1,) * (len(dims) - dim - 1))

    loudness = one(*pieces[0])
    for cut in pieces[1:]:
        loudness = loudness * one(*cut)
    return loudness


def normal_values(own_key, dims, spread, bound, cuts=(), held_as=jnp.bfloat16):
    entries = spread * jax.random.normal(own_key, dims, jnp.float32)
    if cuts:
        entries = entries * shard_levels(own_key, dims, cuts, -0.22, 0.18)
    return jnp.clip(entries, -bound, bound).astype(held_as)


def setup_inputs(seed: int = 0) -> dict:
    arg_keys = jax.random.split(jax.random.key(seed), 4)
    return {
        "projections": normal_values(arg_keys[0], (NPROJ, NV, NU), 4.0, 16.0, ((0, 8), (1, 16))),
        "angle_index": plant(jax.random.randint(arg_keys[1], (NPROJ,), 0, NANG), jax.random.fold_in(arg_keys[1], 1), 0, NANG - 1).astype(jnp.int32),
        "row_ranges": draw_row_ranges(jax.random.fold_in(arg_keys[3], 71), 0),
    }


lower_edge = 0.04
upper_edge = 0.35


def ramp_table():
    offset = jnp.arange(NU, dtype=jnp.int32)[:, None] - jnp.arange(NU, dtype=jnp.int32)[None, :]
    odd_offset = (offset % 2) == 1
    distance = jnp.where(odd_offset, offset, 1).astype(jnp.float32)
    spacing = NX / NU
    values = jnp.where(offset == 0, 0.25, jnp.where(odd_offset, -1.0 / (math.pi * math.pi * distance * distance), 0.0))
    return (values / spacing).astype(jnp.bfloat16)


def sample_rows(sines, depth_first, depth_count, depth_total):
    number = sines.shape[0]
    depth_place = (depth_first + jnp.arange(depth_count, dtype=jnp.int32)).astype(jnp.float32)
    tilt_factor = (2.0 * depth_place - (depth_total - 1)) / (depth_total - 1)
    offset_rows = 0.5 + (HALO - 1) * sines[:, None] * tilt_factor[None, :]
    floor_part = jnp.floor(offset_rows)
    fraction = offset_rows - floor_part
    row_index = HALO + floor_part.astype(jnp.int32)[:, :, None] + 2 * jnp.arange(YB_DEV, dtype=jnp.int32)[None, None, :]
    row_index = row_index.reshape(number, depth_count * YB_DEV)
    fraction = jnp.broadcast_to(fraction[:, :, None], (number, depth_count, YB_DEV)).reshape(number, depth_count * YB_DEV)
    return row_index, fraction


def column_weights(cosines, block_index):
    block_width = min(128, NX)
    band_width = (NU // NX) * block_width
    x_place = (block_index * block_width + jnp.arange(block_width, dtype=jnp.int32)).astype(jnp.float32)
    column = (NU - 1) / 2.0 + (NU / NX) * cosines[:, None] * (x_place[None, :] - (NX - 1) / 2.0)
    first_column = jnp.minimum(column[:, 0], column[:, -1])
    band_start = jnp.clip(jnp.floor(first_column), 0, NU - band_width).astype(jnp.int32)
    columns = (band_start[:, None] + jnp.arange(band_width, dtype=jnp.int32)[None, :]).astype(jnp.float32)
    weights = jnp.maximum(0.0, 1.0 - jnp.abs(columns[:, :, None] - column[:, None, :]))
    return band_start, weights.astype(jnp.bfloat16)


def slice_band(extended_rows, band_start):
    return lax.dynamic_slice_in_dim(extended_rows, band_start, (NU // NX) * min(128, NX), 1)


def take_rows(column_band, row_index):
    return jnp.take(column_band, row_index, axis=0)


def backproject(extended, cosines, sines, depth_first, depth_count, depth_total):
    row_index, fraction = sample_rows(sines, depth_first, depth_count, depth_total)
    block_width = min(128, NX)
    results = []
    for block_index in range(NX // block_width):
        band_start, weights = column_weights(cosines, block_index)
        column_band = jax.vmap(slice_band)(extended, band_start)
        low_rows = jax.vmap(take_rows)(column_band, row_index).astype(jnp.float32)
        high_rows = jax.vmap(take_rows)(column_band, row_index + 1).astype(jnp.float32)
        blended = ((1.0 - fraction)[:, :, None] * low_rows + fraction[:, :, None] * high_rows).astype(jnp.bfloat16)
        results.append(jnp.einsum('pmu,pux->mx', blended.astype(jnp.float32), weights.astype(jnp.float32)))
    return jnp.concatenate(results, axis=1)


def folded_square(indices, number):
    frequency = ((indices + number // 2) % number - number // 2).astype(jnp.float32) / number
    return frequency * frequency


def annulus_gain(radius_square):
    lower_part = (radius_square / (lower_edge * lower_edge)) ** 8
    upper_part = (radius_square / (upper_edge * upper_edge)) ** 8
    return lower_part / (1.0 + lower_part) / (1.0 + upper_part)


def band_response():
    depth_sq = folded_square(jnp.arange(NZ, dtype=jnp.int32), NZ)
    row_sq = folded_square(jnp.arange(NY, dtype=jnp.int32), NY)
    column_sq = folded_square(jnp.arange(NX, dtype=jnp.int32), NX)
    radius_square = depth_sq[:, None, None] + row_sq[None, :, None] + column_sq[None, None, :]
    return annulus_gain(radius_square)


def reference(projections, angle_index, row_ranges):
    filtered = jnp.dot(projections.reshape(-1, NU), ramp_table(), preferred_element_type=jnp.float32)
    filtered = filtered.astype(jnp.bfloat16).reshape(NPROJ, NV, NU)
    padded = jnp.pad(filtered, ((0, 0), (HALO, HALO), (0, 0)))
    angles = 2.0 * math.pi * angle_index.astype(jnp.float32) / NANG
    cosines = jnp.cos(angles)
    sines = jnp.sin(angles)
    scale = math.pi / NPROJ
    extent = RB_DEV + 2 * HALO

    def one_band(band_index):
        extended = lax.dynamic_slice_in_dim(padded, band_index * RB_DEV, extent, 1)
        detector_row = band_index * RB_DEV - HALO + jnp.arange(extent, dtype=jnp.int32)
        limits = row_ranges[band_index]
        accepted = (detector_row >= limits[0]) & (detector_row < limits[1])
        extended = extended * accepted.astype(jnp.bfloat16)[None, :, None]
        running = jnp.zeros((NZ * YB_DEV, NX), jnp.float32)
        for group_index in range(N_DEPTH):
            first_row = group_index * NP_DEV
            last_row = first_row + NP_DEV
            portion = backproject(extended[first_row:last_row], cosines[first_row:last_row], sines[first_row:last_row], 0, NZ, NZ) * scale
            running = running + lax.optimization_barrier(portion.astype(jnp.bfloat16)).astype(jnp.float32)
        return running.reshape(NZ, YB_DEV, NX)

    bands = lax.map(one_band, jnp.arange(N_YBAND, dtype=jnp.int32))
    volume = jnp.transpose(bands, (1, 0, 2, 3)).reshape(NZ, NY, NX)
    spectrum = jnp.fft.fftn(volume)
    banded = jnp.real(jnp.fft.ifftn(spectrum * band_response()))
    return banded.astype(jnp.float32)
```

```python
import math

import jax
import jax.numpy as jnp
import numpy as np
from jax import lax
from jax.experimental import pallas as pl
from jax.experimental.pallas import tpu as pltpu
from jax.sharding import PartitionSpec as P

NX, NU, NANG, NY, NZ = 1024, 2048, 1440, 128, 128
NP_DEV, YB, RB, HALO, BANDS, NPROJ = 2, 8, 16, 12, 16, 16
N = 128
KX = NX // N
MESH = pl.DeviceIdType.MESH
highest = lax.Precision.HIGHEST
lower_edge, upper_edge = 0.04, 0.35


def real_basis(n):
    t = np.arange(n)
    rows = np.arange(n)
    k = np.where(rows <= n // 2, rows, rows - n // 2)
    ph = 2.0 * np.pi * ((k[:, None] * t[None, :]) % n) / n
    q = np.where((rows <= n // 2)[:, None], np.cos(ph), np.sin(ph))
    norm = np.where((rows == 0) | (rows == n // 2), 1.0 / n, 2.0 / n)
    return q * np.sqrt(norm)[:, None], k


def ramp_values():
    n = np.arange(-(NU - 1), NU)
    odd = n % 2 != 0
    d = np.where(odd, n, 1).astype(np.float32)
    v = np.where(n == 0, np.float32(0.25), np.where(odd, np.float32(-1.0) / (np.float32(math.pi * math.pi) * d * d), np.float32(0)))
    return (v / np.float32(NX / NU)).astype(jnp.bfloat16)


def exchange(x, cid, name):
    def kernel(x_ref, o_ref, ss, rs):
        me = lax.axis_index("depth") * BANDS + lax.axis_index("yband")

        def place(o):
            t = (me + o) & (N - 1)
            return t, (t >> 4, t & 15)

        bar = pltpu.get_barrier_semaphore()

        def greet(o, c):
            pl.semaphore_signal(bar, inc=1, device_id=place(o)[1], device_id_type=MESH)
            return c

        lax.fori_loop(1, N, greet, 0)
        pl.semaphore_wait(bar, N - 1)

        def send(o, c):
            t, dev = place(o)
            pltpu.make_async_remote_copy(x_ref.at[t], o_ref.at[me], ss, rs, device_id=dev, device_id_type=MESH).start()
            return c

        lax.fori_loop(1, N, send, 0)
        o_ref[me] = x_ref[me]
        pltpu.make_async_copy(x_ref.at[pl.ds(0, N - 1)], x_ref.at[pl.ds(0, N - 1)], ss).wait()
        pltpu.make_async_copy(o_ref.at[pl.ds(0, N - 1)], o_ref.at[pl.ds(0, N - 1)], rs).wait()

    return pl.pallas_call(
        kernel,
        name=name,
        out_shape=jax.ShapeDtypeStruct(x.shape, x.dtype),
        in_specs=[pl.BlockSpec(memory_space=pltpu.VMEM)],
        out_specs=pl.BlockSpec(memory_space=pltpu.VMEM),
        scratch_shapes=[pltpu.SemaphoreType.DMA, pltpu.SemaphoreType.DMA],
        compiler_params=pltpu.CompilerParams(collective_id=cid, has_side_effects=True, vmem_limit_bytes=16 * 2**20),
    )(x)


def on_device(projections, angle_index, row_ranges):
    d = lax.axis_index("depth")
    b = lax.axis_index("yband")
    me = d * BANDS + b
    theta = 2.0 * math.pi * angle_index.astype(jnp.float32) / NANG
    cosines, sines = jnp.cos(theta), jnp.sin(theta)
    qx, kx = real_basis(NX)
    qy, ky = real_basis(NY)
    qz, kz = real_basis(NZ)
    v = ramp_values()
    idx = np.arange(NU)[:, None] - np.arange(NU)[None, :] + NU - 1
    ramp = jnp.asarray(v[idx])
    filtered = jnp.dot(projections.reshape(-1, NU), ramp, preferred_element_type=jnp.float32)
    filtered = filtered.astype(jnp.bfloat16).reshape(NP_DEV, RB, NU)
    cos_own = lax.dynamic_slice_in_dim(cosines, d * NP_DEV, NP_DEV)
    x = jnp.arange(NX, dtype=jnp.float32)
    column = (NU - 1) / 2.0 + NU / NX * cos_own[:, None] * (x[None, :] - (NX - 1) / 2.0)
    u = jnp.arange(NU, dtype=jnp.float32)
    w = jnp.maximum(0.0, 1.0 - jnp.abs(u[None, :, None] - column[:, None, :])).astype(jnp.bfloat16)
    g = jnp.einsum("pgu,pux->pgx", filtered, w, preferred_element_type=jnp.float32).reshape(32, NX)
    perm = (np.arange(N)[None, :] * KX + np.arange(KX)[:, None]).reshape(-1)
    qxf = jnp.asarray(qx.T[:, perm].astype(np.float32))
    ghat = jnp.dot(g, qxf, precision=highest)
    s = ghat.reshape(32, KX, N).transpose(2, 1, 0).reshape(N, 256)
    lane = jnp.arange(128)
    lim = jnp.where(lane < 64, row_ranges[0, 0], row_ranges[0, 1])
    lim = jnp.where(lane % 16 == b, lim, 0).astype(jnp.float32)
    s = jnp.concatenate([s, jnp.broadcast_to(lim[None], (N, 128))], axis=1)
    r = exchange(s.reshape(N, 1, 384), 1, "spectra").reshape(N, 384)
    lims = r[:16, 256:].sum(0)
    lo = jnp.tile(lims[:16], KX)
    hi = jnp.tile(lims[64:80], KX)
    dd = r[:, :256].reshape(8, BANDS, KX, 32).transpose(0, 3, 2, 1).reshape(256, 128)
    grow = jnp.tile(jnp.arange(16), 16)
    blocks = []
    for sh in (-1, 0, 1):
        row = (16 * (jnp.tile(jnp.arange(16), KX)[None, :] + sh) + grow[:, None]).astype(jnp.float32)
        ok = (row >= lo) & (row < hi) & (row >= 0) & (row < 256)
        blocks.append(jnp.where(ok, jnp.roll(dd, -sh, axis=1), 0.0))
    dext = jnp.concatenate(blocks, axis=0).astype(jnp.bfloat16)
    sin_l = jnp.tile(jnp.repeat(sines, 16), 3)
    c_l = (16 * (jnp.arange(768) // 256) - 16 + jnp.arange(768) % 16).astype(jnp.float32)
    tilt = (2.0 * jnp.arange(NZ, dtype=jnp.float32) - (NZ - 1)) / (NZ - 1)
    e = c_l[None] - (0.5 + (HALO - 1) * sin_l[None] * tilt[:, None])
    parts = []
    for yy in range(YB):
        rm = jnp.maximum(0.0, 1.0 - jnp.abs(e - 2.0 * yy)).astype(jnp.bfloat16)
        parts.append(jnp.dot(rm, dext, preferred_element_type=jnp.float32))
    vol = jnp.concatenate(parts, axis=1)
    bt = np.zeros((YB, KX, BANDS, KX, NY))
    for kk in range(KX):
        bt[:, kk, :, kk, :] = qy.reshape(NY, BANDS, YB).transpose(2, 1, 0)
    bt = jnp.asarray(bt.reshape(1024, 1024).astype(np.float32))
    t1 = jnp.dot(vol, bt, precision=highest)
    qzc = jnp.asarray(qz.astype(np.float32))
    t2 = jnp.dot(qzc, t1, precision=highest)
    row = me * KX + jnp.arange(KX)
    fx = (jnp.where(row <= NX // 2, row, row - NX // 2).astype(jnp.float32) / NX) ** 2
    fy = jnp.asarray(((ky / NY) ** 2).astype(np.float32))
    fz = jnp.asarray(((kz / NZ) ** 2).astype(np.float32))
    rad = fz[:, None] + (fx[:, None] + fy[None, :]).reshape(1, 1024)
    low = (rad / (lower_edge * lower_edge)) ** 8
    up = (rad / (upper_edge * upper_edge)) ** 8
    gain = low / (1.0 + low) / (1.0 + up) * (math.pi / NPROJ)
    t3 = jnp.dot(qzc.T, t2 * gain, precision=highest)
    t4 = jnp.einsum("zkj,jy->zky", t3.reshape(NZ, KX, NY), jnp.asarray(qy.astype(np.float32)), precision=highest)
    back = exchange(t4.astype(jnp.bfloat16), 2, "volume").reshape(NX, NY)
    out = lax.dot_general(back.astype(jnp.float32), jnp.asarray(qx.astype(np.float32)), (((0,), (0,)), ((), ())), precision=highest)
    return out[None]


def solution(mesh):
    return jax.shard_map(
        on_device,
        mesh=mesh,
        in_specs=(P("depth", "yband", None), P(), P("yband", None)),
        out_specs=P(("depth", "yband"), None, None),
        check_vma=False,
    )
```

```python
import math

import jax
import jax.numpy as jnp
import numpy as np
from jax import lax
from jax.experimental import pallas as pl
from jax.experimental.pallas import tpu as pltpu
from jax.sharding import PartitionSpec as P

NX, NU, NANG, NY, NZ = 1024, 2048, 1440, 128, 128
NP_DEV, YB, RB, HALO, BANDS, NPROJ = 2, 8, 16, 12, 16, 16
N = 128
KX = NX // N
ROWS = NP_DEV * RB
TILE = 256
WIN = 384
MESH = pl.DeviceIdType.MESH
lower_edge, upper_edge = 0.04, 0.35
f32, bf16 = jnp.float32, jnp.bfloat16


def real_basis(n):
    rows = np.arange(n)
    k = np.where(rows <= n // 2, rows, rows - n // 2)
    phase = 2.0 * np.pi * ((k[:, None] * rows[None, :]) % n) / n
    q = np.where((rows <= n // 2)[:, None], np.cos(phase), np.sin(phase))
    norm = np.where((rows == 0) | (rows == n // 2), 1.0 / n, 2.0 / n)
    return q * np.sqrt(norm)[:, None]


def ramp_tiles():
    n = np.arange(-(NU - 1), NU)
    odd = n % 2 != 0
    dist = np.where(odd, n, 1).astype(np.float32)
    values = np.where(n == 0, np.float32(0.25), np.where(odd, np.float32(-1.0) / (np.float32(math.pi * math.pi) * dist * dist), np.float32(0)))
    values = (values / np.float32(NX / NU)).astype(bf16)
    blocks = NU // TILE
    off = np.arange(1 - blocks, blocks)[:, None, None] * TILE
    at = off + np.arange(TILE)[None, :, None] - np.arange(TILE)[None, None, :]
    return values[at + NU - 1]


def tables():
    qx, qy, qz = real_basis(NX), real_basis(NY), real_basis(NZ)
    order = (np.arange(N)[None, :] * KX + np.arange(KX)[:, None]).reshape(-1)
    forward_x = qx.T[:, order]
    bands = np.zeros((YB, KX, BANDS, KX, NY))
    for k in range(KX):
        bands[:, k, :, k, :] = qy.reshape(NY, BANDS, YB).transpose(2, 1, 0)
    small = np.stack([qz, qz.T, qy])
    angle = (np.float32(2.0 * math.pi) * np.arange(NANG, dtype=np.float32) / np.float32(NANG)).astype(np.float64)
    trig = np.concatenate([np.cos(angle), np.sin(angle)]).astype(np.float32)
    return (
        jnp.asarray(ramp_tiles()),
        jnp.asarray(forward_x.astype(np.float32), bf16),
        jnp.asarray(bands.reshape(YB * KX * BANDS, KX * NY).astype(np.float32), bf16),
        jnp.asarray(qx.astype(np.float32), bf16),
        jnp.asarray(small.astype(np.float32), bf16),
        jnp.asarray(trig),
    )


def iota(shape, axis):
    return lax.broadcasted_iota(jnp.int32, shape, axis)


def dot(a, b):
    return jnp.dot(a, b, preferred_element_type=f32)


def fold_freq(row, n):
    k = jnp.where(row <= n // 2, row, row - n // 2).astype(f32) / n
    return k * k


def kernel(
    angle_ref, limit_ref, trig_ref, proj_ref,
    ramp_hbm, forward_hbm, bands_hbm, inverse_hbm, small_hbm,
    out_ref,
    ramp_ref, forward_ref, bands_ref, inverse_ref, small_ref,
    stack_ref, filt_ref, g_ref, send1, recv1, rows_ref, gain_ref, vol_ref, mix_ref, send2, recv2,
    table_sems, send_sems, recv_sems,
):
    d = lax.axis_index("depth")
    b = lax.axis_index("yband")
    me = d * BANDS + b

    def place(o):
        t = (me + o) & (N - 1)
        return t, (t >> 4, t & 15)

    loads = [
        pltpu.make_async_copy(src, dst, table_sems.at[i])
        for i, (src, dst) in enumerate(
            [(ramp_hbm, ramp_ref), (forward_hbm, forward_ref), (small_hbm, small_ref), (bands_hbm, bands_ref), (inverse_hbm, inverse_ref)]
        )
    ]
    for load in loads:
        load.start()

    bar = pltpu.get_barrier_semaphore()

    def greet(o, c):
        pl.semaphore_signal(bar, inc=1, device_id=place(o)[1], device_id_type=MESH)
        return c

    lax.fori_loop(1, N, greet, 0, unroll=True)

    blocks = NU // TILE
    for i in range(blocks):
        stack_ref[i * ROWS : (i + 1) * ROWS, :] = proj_ref[:, i * TILE : (i + 1) * TILE]
    loads[0].wait()
    acc = [jnp.zeros((ROWS, TILE), f32) for _ in range(blocks)]
    for k in range(1 - blocks, blocks):
        first, last = max(k, 0), blocks + min(k, 0)
        part = dot(stack_ref[first * ROWS : last * ROWS, :], ramp_ref[k + blocks - 1])
        for i in range(first, last):
            acc[i - k] += part[(i - first) * ROWS : (i - first + 1) * ROWS]
    for j in range(blocks):
        filt_ref[:, j * TILE : (j + 1) * TILE] = acc[j].astype(bf16)

    sub = iota((WIN, N), 0).astype(f32)
    lane_x = iota((1, N), 1).astype(f32)
    for p in range(NP_DEV):
        slope = jnp.full((1, N), 2.0 * trig_ref[angle_ref[d * NP_DEV + p]])
        rows = [filt_ref[p * RB : (p + 1) * RB, i * N : (i + 1) * N] for i in range(NU // N)]
        for i in range(NX // N):
            column = (NU - 1) / 2.0 + slope * ((lane_x + float(i * N)) - (NX - 1) / 2.0)
            ends = [(NU - 1) / 2.0 + slope * (i * N + end - (NX - 1) / 2.0) for end in (0.0, N - 1.0)]
            tile = jnp.clip(jnp.floor(jnp.minimum(ends[0], ends[1]) * (1.0 / N)), 0.0, float((NU - WIN) // N))
            column = column - tile * float(N)
            weights = jnp.maximum(0.0, 1.0 - jnp.abs(sub - column)).astype(bf16)
            window = rows
            for bit in (8, 4, 2, 1):
                up = tile >= float(bit)
                tile = jnp.where(up, tile - float(bit), tile)
                upper = jnp.broadcast_to(up, (RB, N))
                keep = bit - 1 + WIN // N
                window = [jnp.where(upper, window[k + bit], window[k]) if k + bit < len(window) else window[k] for k in range(keep)]
            g_ref[p * RB : (p + 1) * RB, i * N : (i + 1) * N] = dot(jnp.concatenate(window, axis=1), weights)

    g = g_ref[...]
    g_high = g.astype(bf16)
    g_low = (g - g_high.astype(f32)).astype(bf16)
    loads[1].wait()
    both = dot(jnp.concatenate([g_high, g_low], axis=0), forward_ref[...])
    spectrum = both[:ROWS] + both[ROWS:]
    for half in range(2):
        tall = jnp.concatenate([spectrum[:, k * N : (k + 1) * N] for k in range(4 * half, 4 * half + 4)], axis=0)
        send1[:, 0, half * N : (half + 1) * N] = tall.T
    lane = iota((N, N), 1)
    limits = jnp.where(lane < 64, limit_ref[0, 0], limit_ref[0, 1])
    send1[:, 0, 2 * N : 3 * N] = jnp.where((lane & 15) == b, limits, 0).astype(f32)

    def exchange(src, dst, s):
        def send(o, c):
            t, dev = place(o)
            pltpu.make_async_remote_copy(src.at[t], dst.at[me], send_sems.at[s], recv_sems.at[s], device_id=dev, device_id_type=MESH).start()
            return c

        lax.fori_loop(1, N, send, 0)
        dst[me] = src[me]

    def arrived(src, dst, s):
        view = dst.at[pl.ds(0, N - 1)]
        pltpu.make_async_copy(view, view, recv_sems.at[s]).wait()
        view = src.at[pl.ds(0, N - 1)]
        pltpu.make_async_copy(view, view, send_sems.at[s]).wait()

    pl.semaphore_wait(bar, N - 1)
    exchange(send1, recv1, 0)

    lanes = iota((1, 3 * 256), 1)
    proj = (lanes & 255) >> 4
    sines = jnp.zeros((1, 3 * 256), f32)
    for p in range(NPROJ):
        sines = jnp.where(proj == p, trig_ref[NANG + angle_ref[p]], sines)
    row_at = (16 * (lanes >> 8) - 16 + (lanes & 15)).astype(f32)
    tilt = (2.0 * iota((NZ, 1), 0).astype(f32) - (NZ - 1)) / (NZ - 1)
    away = row_at - (0.5 + (HALO - 1) * sines * tilt)
    for y in range(YB):
        rows_ref[y] = jnp.maximum(0.0, 1.0 - jnp.abs(away - 2.0 * y)).astype(bf16)
    fz = fold_freq(iota((NZ, 1), 0), NZ)
    fy = fold_freq(iota((1, NY), 1), NY)
    for k in range(KX):
        fx = fold_freq(me * KX + k + iota((1, NY), 1) * 0, NX)
        radius = fz + (fx + fy)
        low = (radius * (1.0 / (lower_edge * lower_edge))) ** 8
        up = (radius * (1.0 / (upper_edge * upper_edge))) ** 8
        gain_ref[:, k * NY : (k + 1) * NY] = low * (math.pi / NPROJ) / ((1.0 + low) * (1.0 + up))

    arrived(send1, recv1, 0)
    x = []
    for half in range(2):
        flat = recv1[:, 0, half * N : (half + 1) * N].T
        x += [flat[k * ROWS : (k + 1) * ROWS] for k in range(4)]
    group = iota((ROWS, N), 1) >> 4
    for bit in (1, 2, 4):
        clear = (group & bit) == 0
        for k in range(KX):
            if k & bit == 0:
                a, c = x[k], x[k + bit]
                x[k] = jnp.where(clear, a, pltpu.roll(c, 16 * bit, 1))
                x[k + bit] = jnp.where(clear, pltpu.roll(a, N - 16 * bit, 1), c)
    data = jnp.concatenate(x, axis=0)
    lims = jnp.sum(recv1[0:BANDS, 0, 2 * N : 3 * N], axis=0, keepdims=True)
    lane1 = iota((1, N), 1)
    swapped = pltpu.roll(lims, 64, 1)
    lo = jnp.where(lane1 < 64, lims, swapped)
    hi = jnp.where(lane1 < 64, swapped, lims)
    pieces = []
    for s in (-1, 0, 1):
        row = (16 * ((iota((RB, N), 1) & 15) + s) + iota((RB, N), 0)).astype(f32)
        ok = (row >= lo) & (row < hi) & (row >= 0.0) & (row < 256.0)
        keep = jnp.where(ok, 1.0, 0.0)
        moved = data if s == 0 else pltpu.roll(data, (-s) % N, 1)
        pieces += [(moved[r * RB : (r + 1) * RB] * keep).astype(bf16) for r in range(NPROJ)]
    extended = jnp.concatenate(pieces, axis=0)
    for y in range(YB):
        vol_ref[:, y * N : (y + 1) * N] = dot(rows_ref[y], extended).astype(bf16)
    loads[3].wait()
    loads[2].wait()
    along_y = dot(vol_ref[...], bands_ref[...]).astype(bf16)
    along_z = dot(small_ref[0], along_y) * gain_ref[...]
    back_z = dot(small_ref[1], along_z.astype(bf16)).astype(bf16)
    for k in range(KX):
        mix_ref[:, k, :] = dot(back_z[:, k * NY : (k + 1) * NY], small_ref[2])
    send2[...] = mix_ref[...].astype(bf16)
    exchange(send2, recv2, 1)
    arrived(send2, recv2, 1)
    loads[4].wait()
    tall = recv2[...].astype(f32).reshape(NX, NY)
    wide = jnp.concatenate([tall[i * N : (i + 1) * N].T for i in range(NX // N)], axis=1).astype(bf16)
    out_ref[0] = dot(wide, inverse_ref[...])


def on_device(projections, angle_index, row_ranges):
    ramp, forward, bands, inverse, small, trig = tables()
    smem = pl.BlockSpec(memory_space=pltpu.SMEM)
    vmem = pl.BlockSpec(memory_space=pltpu.VMEM)
    hbm = pl.BlockSpec(memory_space=pl.ANY)
    return pl.pallas_call(
        kernel,
        name="laminograph",
        out_shape=jax.ShapeDtypeStruct((1, NY, NX), f32),
        in_specs=[smem] * 3 + [vmem] + [hbm] * 5,
        out_specs=vmem,
        scratch_shapes=[
            pltpu.VMEM(ramp.shape, bf16),
            pltpu.VMEM(forward.shape, bf16),
            pltpu.VMEM(bands.shape, bf16),
            pltpu.VMEM(inverse.shape, bf16),
            pltpu.VMEM(small.shape, bf16),
            pltpu.VMEM((NU // TILE * ROWS, TILE), bf16),
            pltpu.VMEM((ROWS, NU), bf16),
            pltpu.VMEM((ROWS, NX), f32),
            pltpu.VMEM((N, 1, 3 * N), f32),
            pltpu.VMEM((N, 1, 3 * N), f32),
            pltpu.VMEM((YB, NZ, 3 * 256), bf16),
            pltpu.VMEM((NZ, KX * NY), f32),
            pltpu.VMEM((NZ, YB * N), bf16),
            pltpu.VMEM((NZ, KX, NY), f32),
            pltpu.VMEM((N, KX, NY), bf16),
            pltpu.VMEM((N, KX, NY), bf16),
            pltpu.SemaphoreType.DMA((5,)),
            pltpu.SemaphoreType.DMA((2,)),
            pltpu.SemaphoreType.DMA((2,)),
        ],
        compiler_params=pltpu.CompilerParams(collective_id=1, has_side_effects=True, vmem_limit_bytes=56 * 2**20),
    )(angle_index, row_ranges, trig, projections.reshape(ROWS, NU), ramp, forward, bands, inverse, small)


def solution(mesh):
    return jax.shard_map(
        on_device,
        mesh=mesh,
        in_specs=(P("depth", "yband", None), P(), P("yband", None)),
        out_specs=P(("depth", "yband"), None, None),
        check_vma=False,
    )
```

```python
import math

import jax
import jax.numpy as jnp
import numpy as np
from jax import lax
from jax.experimental import pallas as pl
from jax.experimental.pallas import tpu as pltpu
from jax.sharding import PartitionSpec as P

NX, NU, NANG, NY, NZ = 1024, 2048, 1440, 128, 128
NP_DEV, YB, RB, HALO, BANDS, NPROJ = 2, 8, 16, 12, 16, 16
N = 128
KX = NX // N
ROWS = NP_DEV * RB
TILE = 256
WIN = 384
MESH = pl.DeviceIdType.MESH
lower_edge, upper_edge = 0.04, 0.35
f32, bf16 = jnp.float32, jnp.bfloat16


def far_first():
    steps = [(x, y, z, c) for x in range(4) for y in range(4) for z in range(4) for c in range(2)]
    hops = lambda s: sum(min(q, 4 - q) for q in s[:3])
    return sorted(steps, key=lambda s: (-hops(s), s))[:-2] + [(0, 0, 0, 1)]


STEPS = far_first()


def real_basis(n):
    rows = np.arange(n)
    k = np.where(rows <= n // 2, rows, rows - n // 2)
    phase = 2.0 * np.pi * ((k[:, None] * rows[None, :]) % n) / n
    q = np.where((rows <= n // 2)[:, None], np.cos(phase), np.sin(phase))
    norm = np.where((rows == 0) | (rows == n // 2), 1.0 / n, 2.0 / n)
    return q * np.sqrt(norm)[:, None]


def ramp_tiles():
    n = np.arange(-(NU - 1), NU)
    odd = n % 2 != 0
    dist = np.where(odd, n, 1).astype(np.float32)
    values = np.where(n == 0, np.float32(0.25), np.where(odd, np.float32(-1.0) / (np.float32(math.pi * math.pi) * dist * dist), np.float32(0)))
    values = (values / np.float32(NX / NU)).astype(bf16)
    blocks = NU // TILE
    off = np.arange(1 - blocks, blocks)[:, None, None] * TILE
    at = off + np.arange(TILE)[None, :, None] - np.arange(TILE)[None, None, :]
    return values[at + NU - 1]


def tables():
    qx, qy, qz = real_basis(NX), real_basis(NY), real_basis(NZ)
    order = (np.arange(N)[None, :] * KX + np.arange(KX)[:, None]).reshape(-1)
    forward_x = qx.T[:, order]
    bands = np.zeros((YB, KX, BANDS, KX, NY))
    for k in range(KX):
        bands[:, k, :, k, :] = qy.reshape(NY, BANDS, YB).transpose(2, 1, 0)
    small = np.stack([qz, qz.T, qy])
    angle = (np.float32(2.0 * math.pi) * np.arange(NANG, dtype=np.float32) / np.float32(NANG)).astype(np.float64)
    trig = np.concatenate([np.cos(angle), np.sin(angle)]).astype(np.float32)
    return (
        jnp.asarray(ramp_tiles()),
        jnp.asarray(forward_x.astype(np.float32), bf16),
        jnp.asarray(bands.reshape(YB * KX * BANDS, KX * NY).astype(np.float32), bf16),
        jnp.asarray(qx.astype(np.float32), bf16),
        jnp.asarray(small.astype(np.float32), bf16),
        jnp.asarray(trig),
    )


def iota(shape, axis):
    return lax.broadcasted_iota(jnp.int32, shape, axis)


def dot(a, b):
    return jnp.dot(a, b, preferred_element_type=f32)


def fold_freq(row, n):
    k = jnp.where(row <= n // 2, row, row - n // 2).astype(f32) / n
    return k * k


def kernel(
    angle_ref, limit_ref, trig_ref, proj_ref,
    ramp_hbm, forward_hbm, bands_hbm, small_hbm,
    recv2,
    ramp_ref, forward_ref, bands_ref, small_ref,
    stack_ref, filt_ref, g_ref, send1, recv1, rows_ref, gain_ref, vol_ref, mix_ref, send2,
    table_sems, send_sems, recv_sems,
):
    d = lax.axis_index("depth")
    b = lax.axis_index("yband")
    me = d * BANDS + b

    px, py = ((d >> 2) << 1) | (b >> 3), d & 3
    pz, pc = (b >> 1) & 3, b & 1

    def place(step):
        dx, dy, dz, dc = step
        x, y, z, c = (px + dx) & 3, (py + dy) & 3, (pz + dz) & 3, pc ^ dc
        dd, bb = ((x >> 1) << 2) | y, ((x & 1) << 3) | (z << 1) | c
        return dd * BANDS + bb, (dd, bb)

    loads = [
        pltpu.make_async_copy(src, dst, table_sems.at[i])
        for i, (src, dst) in enumerate(
            [(ramp_hbm, ramp_ref), (forward_hbm, forward_ref), (small_hbm, small_ref), (bands_hbm, bands_ref)]
        )
    ]
    for load in loads:
        load.start()

    bar = pltpu.get_barrier_semaphore()

    for step in STEPS:
        pl.semaphore_signal(bar, inc=1, device_id=place(step)[1], device_id_type=MESH)

    blocks = NU // TILE
    for i in range(blocks):
        stack_ref[i * ROWS : (i + 1) * ROWS, :] = proj_ref[:, i * TILE : (i + 1) * TILE]
    loads[0].wait()
    acc = [jnp.zeros((ROWS, TILE), f32) for _ in range(blocks)]
    for k in range(1 - blocks, blocks):
        first, last = max(k, 0), blocks + min(k, 0)
        part = dot(stack_ref[first * ROWS : last * ROWS, :], ramp_ref[k + blocks - 1])
        for i in range(first, last):
            acc[i - k] += part[(i - first) * ROWS : (i - first + 1) * ROWS]
    for j in range(blocks):
        filt_ref[:, j * TILE : (j + 1) * TILE] = acc[j].astype(bf16)

    sub = iota((WIN, N), 0).astype(f32)
    lane_x = iota((1, N), 1).astype(f32)
    for p in range(NP_DEV):
        slope = jnp.full((1, N), 2.0 * trig_ref[angle_ref[d * NP_DEV + p]])
        rows = [filt_ref[p * RB : (p + 1) * RB, i * N : (i + 1) * N] for i in range(NU // N)]
        for i in range(NX // N):
            column = (NU - 1) / 2.0 + slope * ((lane_x + float(i * N)) - (NX - 1) / 2.0)
            ends = [(NU - 1) / 2.0 + slope * (i * N + end - (NX - 1) / 2.0) for end in (0.0, N - 1.0)]
            tile = jnp.clip(jnp.floor(jnp.minimum(ends[0], ends[1]) * (1.0 / N)), 0.0, float((NU - WIN) // N))
            column = column - tile * float(N)
            weights = jnp.maximum(0.0, 1.0 - jnp.abs(sub - column)).astype(bf16)
            window = rows
            for bit in (8, 4, 2, 1):
                up = tile >= float(bit)
                tile = jnp.where(up, tile - float(bit), tile)
                upper = jnp.broadcast_to(up, (RB, N))
                keep = bit - 1 + WIN // N
                window = [jnp.where(upper, window[k + bit], window[k]) if k + bit < len(window) else window[k] for k in range(keep)]
            g_ref[p * RB : (p + 1) * RB, i * N : (i + 1) * N] = dot(jnp.concatenate(window, axis=1), weights)

    g = g_ref[...]
    g_high = g.astype(bf16)
    g_low = (g - g_high.astype(f32)).astype(bf16)
    loads[1].wait()
    both = dot(jnp.concatenate([g_high, g_low], axis=0), forward_ref[...])
    spectrum = both[:ROWS] + both[ROWS:]
    for half in range(2):
        tall = jnp.concatenate([spectrum[:, k * N : (k + 1) * N] for k in range(4 * half, 4 * half + 4)], axis=0)
        send1[:, 0, half * N : (half + 1) * N] = tall.T
    lane = iota((N, N), 1)
    limits = jnp.where(lane < 64, limit_ref[0, 0], limit_ref[0, 1])
    send1[:, 0, 2 * N : 3 * N] = jnp.where((lane & 15) == b, limits, 0).astype(f32)

    def exchange(src, dst, s):
        for step in STEPS:
            t, dev = place(step)
            pltpu.make_async_remote_copy(src.at[t], dst.at[me], send_sems.at[s], recv_sems.at[s], device_id=dev, device_id_type=MESH).start()
        dst[me] = src[me]

    def arrived(src, dst, s):
        view = dst.at[pl.ds(0, N - 1)]
        pltpu.make_async_copy(view, view, recv_sems.at[s]).wait()

    pl.semaphore_wait(bar, N - 1)
    exchange(send1, recv1, 0)

    lanes = iota((1, 3 * 256), 1)
    proj = (lanes & 255) >> 4
    sines = jnp.zeros((1, 3 * 256), f32)
    for p in range(NPROJ):
        sines = jnp.where(proj == p, trig_ref[NANG + angle_ref[p]], sines)
    row_at = (16 * (lanes >> 8) - 16 + (lanes & 15)).astype(f32)
    tilt = (2.0 * iota((NZ, 1), 0).astype(f32) - (NZ - 1)) / (NZ - 1)
    away = row_at - (0.5 + (HALO - 1) * sines * tilt)
    for y in range(YB):
        rows_ref[y] = jnp.maximum(0.0, 1.0 - jnp.abs(away - 2.0 * y)).astype(bf16)
    fz = fold_freq(iota((NZ, 1), 0), NZ)
    fy = fold_freq(iota((1, NY), 1), NY)
    for k in range(KX):
        fx = fold_freq(me * KX + k + iota((1, NY), 1) * 0, NX)
        radius = fz + (fx + fy)
        low = (radius * (1.0 / (lower_edge * lower_edge))) ** 8
        up = (radius * (1.0 / (upper_edge * upper_edge))) ** 8
        gain_ref[:, k * NY : (k + 1) * NY] = low * (math.pi / NPROJ) / ((1.0 + low) * (1.0 + up))

    arrived(send1, recv1, 0)
    x = []
    for half in range(2):
        flat = recv1[:, 0, half * N : (half + 1) * N].T
        x += [flat[k * ROWS : (k + 1) * ROWS] for k in range(4)]
    group = iota((ROWS, N), 1) >> 4
    for bit in (1, 2, 4):
        clear = (group & bit) == 0
        for k in range(KX):
            if k & bit == 0:
                a, c = x[k], x[k + bit]
                x[k] = jnp.where(clear, a, pltpu.roll(c, 16 * bit, 1))
                x[k + bit] = jnp.where(clear, pltpu.roll(a, N - 16 * bit, 1), c)
    data = jnp.concatenate(x, axis=0)
    lims = jnp.sum(recv1[0:BANDS, 0, 2 * N : 3 * N], axis=0, keepdims=True)
    lane1 = iota((1, N), 1)
    swapped = pltpu.roll(lims, 64, 1)
    lo = jnp.where(lane1 < 64, lims, swapped)
    hi = jnp.where(lane1 < 64, swapped, lims)
    pieces = []
    for s in (-1, 0, 1):
        row = (16 * ((iota((RB, N), 1) & 15) + s) + iota((RB, N), 0)).astype(f32)
        ok = (row >= lo) & (row < hi) & (row >= 0.0) & (row < 256.0)
        keep = jnp.where(ok, 1.0, 0.0)
        moved = data if s == 0 else pltpu.roll(data, (-s) % N, 1)
        pieces += [(moved[r * RB : (r + 1) * RB] * keep).astype(bf16) for r in range(NPROJ)]
    extended = jnp.concatenate(pieces, axis=0)
    for y in range(YB):
        vol_ref[:, y * N : (y + 1) * N] = dot(rows_ref[y], extended).astype(bf16)
    loads[3].wait()
    loads[2].wait()
    along_y = dot(vol_ref[...], bands_ref[...]).astype(bf16)
    along_z = dot(small_ref[0], along_y) * gain_ref[...]
    back_z = dot(small_ref[1], along_z.astype(bf16)).astype(bf16)
    for k in range(KX):
        mix_ref[:, k, :] = dot(back_z[:, k * NY : (k + 1) * NY], small_ref[2])
    send2[...] = mix_ref[...].astype(bf16)
    exchange(send2, recv2, 1)
    arrived(send2, recv2, 1)
    for s, src in enumerate((send1, send2)):
        view = src.at[pl.ds(0, N - 1)]
        pltpu.make_async_copy(view, view, send_sems.at[s]).wait()


def on_device(projections, angle_index, row_ranges):
    ramp, forward, bands, inverse, small, trig = tables()
    smem = pl.BlockSpec(memory_space=pltpu.SMEM)
    vmem = pl.BlockSpec(memory_space=pltpu.VMEM)
    hbm = pl.BlockSpec(memory_space=pl.ANY)
    back = pl.pallas_call(
        kernel,
        name="laminograph",
        out_shape=jax.ShapeDtypeStruct((N, KX, NY), bf16),
        in_specs=[smem] * 3 + [vmem] + [hbm] * 4,
        out_specs=vmem,
        scratch_shapes=[
            pltpu.VMEM(ramp.shape, bf16),
            pltpu.VMEM(forward.shape, bf16),
            pltpu.VMEM(bands.shape, bf16),
            pltpu.VMEM(small.shape, bf16),
            pltpu.VMEM((NU // TILE * ROWS, TILE), bf16),
            pltpu.VMEM((ROWS, NU), bf16),
            pltpu.VMEM((ROWS, NX), f32),
            pltpu.VMEM((N, 1, 3 * N), f32),
            pltpu.VMEM((N, 1, 3 * N), f32),
            pltpu.VMEM((YB, NZ, 3 * 256), bf16),
            pltpu.VMEM((NZ, KX * NY), f32),
            pltpu.VMEM((NZ, YB * N), bf16),
            pltpu.VMEM((NZ, KX, NY), f32),
            pltpu.VMEM((N, KX, NY), bf16),
            pltpu.SemaphoreType.DMA((4,)),
            pltpu.SemaphoreType.DMA((2,)),
            pltpu.SemaphoreType.DMA((2,)),
        ],
        compiler_params=pltpu.CompilerParams(collective_id=1, has_side_effects=True, vmem_limit_bytes=56 * 2**20),
    )(angle_index, row_ranges, trig, projections.reshape(ROWS, NU), ramp, forward, bands, small)
    return lax.dot_general(back.reshape(NX, NY), inverse, (((0,), (0,)), ((), ())), preferred_element_type=f32)[None]


def solution(mesh):
    return jax.shard_map(
        on_device,
        mesh=mesh,
        in_specs=(P("depth", "yband", None), P(), P("yband", None)),
        out_specs=P(("depth", "yband"), None, None),
        check_vma=False,
    )
```

```python
import math

import jax
import jax.numpy as jnp
import numpy as np
from jax import lax
from jax.experimental import pallas as pl
from jax.experimental.pallas import tpu as pltpu
from jax.sharding import PartitionSpec as P

NX, NU, NANG, NY, NZ = 1024, 2048, 1440, 128, 128
NP_DEV, YB, RB, HALO, BANDS, NPROJ = 2, 8, 16, 12, 16, 16
N = 128
KX = NX // N
ROWS = NP_DEV * RB
TILE = 256
WIN = 384
MESH = pl.DeviceIdType.MESH
lower_edge, upper_edge = 0.04, 0.35
f32, bf16 = jnp.float32, jnp.bfloat16


def far_first():
    steps = [(x, y, z, c) for x in range(4) for y in range(4) for z in range(4) for c in range(2)]
    hops = lambda s: sum(min(q, 4 - q) for q in s[:3])
    return sorted(steps, key=lambda s: (-hops(s), s))[:-2] + [(0, 0, 0, 1)]


def far_chunks():
    chunks = []
    for high, y in sorted([(h, y) for h in range(2) for y in range(4)], key=lambda q: (-2 * q[0] - min(q[1], 4 - q[1]), q)):
        inner = [(low, z, c) for low in range(2) for z in range(4) for c in range(2)]
        inner.sort(key=lambda q: (-abs(2 * high - q[0]) - min(q[1], 4 - q[1]), q))
        chunks.append([(high, low, y, z, c) for low, z, c in inner])
    return chunks


STEPS = far_first()
CHUNKS = far_chunks()


def real_basis(n):
    rows = np.arange(n)
    k = np.where(rows <= n // 2, rows, rows - n // 2)
    phase = 2.0 * np.pi * ((k[:, None] * rows[None, :]) % n) / n
    q = np.where((rows <= n // 2)[:, None], np.cos(phase), np.sin(phase))
    norm = np.where((rows == 0) | (rows == n // 2), 1.0 / n, 2.0 / n)
    return q * np.sqrt(norm)[:, None]


def ramp_tiles():
    n = np.arange(-(NU - 1), NU)
    odd = n % 2 != 0
    dist = np.where(odd, n, 1).astype(np.float32)
    values = np.where(n == 0, np.float32(0.25), np.where(odd, np.float32(-1.0) / (np.float32(math.pi * math.pi) * dist * dist), np.float32(0)))
    values = (values / np.float32(NX / NU)).astype(bf16)
    blocks = NU // TILE
    off = np.arange(1 - blocks, blocks)[:, None, None] * TILE
    at = off + np.arange(TILE)[None, :, None] - np.arange(TILE)[None, None, :]
    return values[at + NU - 1]


def tables():
    qx, qy, qz = real_basis(NX), real_basis(NY), real_basis(NZ)
    order = (np.arange(N)[None, :] * KX + np.arange(KX)[:, None]).reshape(-1)
    forward_x = qx.T[:, order]
    bands = np.zeros((YB, KX, BANDS, KX, NY))
    for k in range(KX):
        bands[:, k, :, k, :] = qy.reshape(NY, BANDS, YB).transpose(2, 1, 0)
    small = np.stack([qz, qz.T, qy])
    angle = (np.float32(2.0 * math.pi) * np.arange(NANG, dtype=np.float32) / np.float32(NANG)).astype(np.float64)
    trig = np.concatenate([np.cos(angle), np.sin(angle)]).astype(np.float32)
    return (
        jnp.asarray(ramp_tiles()),
        jnp.asarray(forward_x.astype(np.float32), bf16),
        jnp.asarray(bands.reshape(YB * KX * BANDS, KX * NY).astype(np.float32), bf16),
        jnp.asarray(qx.astype(np.float32), bf16),
        jnp.asarray(small.astype(np.float32), bf16),
        jnp.asarray(trig),
    )


def iota(shape, axis):
    return lax.broadcasted_iota(jnp.int32, shape, axis)


def dot(a, b):
    return jnp.dot(a, b, preferred_element_type=f32)


def fold_freq(row, n):
    k = jnp.where(row <= n // 2, row, row - n // 2).astype(f32) / n
    return k * k


def kernel(
    angle_hbm, limit_hbm, trig_hbm, proj_hbm, ramp_hbm, forward_hbm, bands_hbm, small_hbm,
    recv2,
    angle_ref, limit_ref, trig_ref, proj_ref, ramp_ref, forward_ref, bands_ref, small_ref,
    stack_ref, filt_ref, g_ref, send1, recv1, rows_ref, gain_ref, vol_ref, back_ref, mix_ref, send2,
    table_sems, send_sems, recv_sems,
):
    d = lax.axis_index("depth")
    b = lax.axis_index("yband")
    me = d * BANDS + b

    px, py = ((d >> 2) << 1) | (b >> 3), d & 3
    pz, pc = (b >> 1) & 3, b & 1

    def place(step):
        dx, dy, dz, dc = step
        x, y, z, c = (px + dx) & 3, (py + dy) & 3, (pz + dz) & 3, pc ^ dc
        dd, bb = ((x >> 1) << 2) | y, ((x & 1) << 3) | (z << 1) | c
        return dd * BANDS + bb, (dd, bb)

    def place2(step):
        high, low, y, z, c = step
        dd = (((d >> 2) ^ high) << 2) | ((py + y) & 3)
        bb = (((b >> 3) ^ low) << 3) | (((pz + z) & 3) << 1) | (pc ^ c)
        return dd * BANDS + bb, (dd, bb)

    pairs = [(proj_hbm, proj_ref), (ramp_hbm, ramp_ref), (angle_hbm, angle_ref), (trig_hbm, trig_ref), (limit_hbm, limit_ref)]
    pairs += [(forward_hbm, forward_ref), (small_hbm, small_ref), (bands_hbm, bands_ref)]
    loads = [pltpu.make_async_copy(src, dst, table_sems.at[i]) for i, (src, dst) in enumerate(pairs)]
    for i in (0, 1, 5):
        loads[i].start()

    bar = pltpu.get_barrier_semaphore()

    for step in STEPS:
        pl.semaphore_signal(bar, inc=1, device_id=place(step)[1], device_id_type=MESH)

    for i in (2, 3, 4, 6, 7):
        loads[i].start()

    blocks = NU // TILE
    loads[0].wait()
    for i in range(blocks):
        stack_ref[i * ROWS : (i + 1) * ROWS, :] = proj_ref[:, i * TILE : (i + 1) * TILE]
    loads[1].wait()
    acc = [jnp.zeros((ROWS, TILE), f32) for _ in range(blocks)]
    for k in range(1 - blocks, blocks):
        first, last = max(k, 0), blocks + min(k, 0)
        part = dot(stack_ref[first * ROWS : last * ROWS, :], ramp_ref[k + blocks - 1])
        for i in range(first, last):
            acc[i - k] += part[(i - first) * ROWS : (i - first + 1) * ROWS]
    for j in range(blocks):
        filt_ref[:, j * TILE : (j + 1) * TILE] = acc[j].astype(bf16)

    for load in loads[2:5]:
        load.wait()
    sub = iota((WIN, N), 0).astype(f32)
    lane_x = iota((1, N), 1).astype(f32)
    for p in range(NP_DEV):
        slope = jnp.full((1, N), 2.0 * trig_ref[angle_ref[d * NP_DEV + p]])
        rows = [filt_ref[p * RB : (p + 1) * RB, i * N : (i + 1) * N] for i in range(NU // N)]
        for i in range(NX // N):
            column = (NU - 1) / 2.0 + slope * ((lane_x + float(i * N)) - (NX - 1) / 2.0)
            ends = [(NU - 1) / 2.0 + slope * (i * N + end - (NX - 1) / 2.0) for end in (0.0, N - 1.0)]
            tile = jnp.clip(jnp.floor(jnp.minimum(ends[0], ends[1]) * (1.0 / N)), 0.0, float((NU - WIN) // N))
            column = column - tile * float(N)
            weights = jnp.maximum(0.0, 1.0 - jnp.abs(sub - column)).astype(bf16)
            window = rows
            for bit in (8, 4, 2, 1):
                up = tile >= float(bit)
                tile = jnp.where(up, tile - float(bit), tile)
                upper = jnp.broadcast_to(up, (RB, N))
                keep = bit - 1 + WIN // N
                window = [jnp.where(upper, window[k + bit], window[k]) if k + bit < len(window) else window[k] for k in range(keep)]
            g_ref[p * RB : (p + 1) * RB, i * N : (i + 1) * N] = dot(jnp.concatenate(window, axis=1), weights)

    g = g_ref[...]
    g_high = g.astype(bf16)
    g_low = (g - g_high.astype(f32)).astype(bf16)
    loads[5].wait()
    both = dot(jnp.concatenate([g_high, g_low], axis=0), forward_ref[...])
    spectrum = both[:ROWS] + both[ROWS:]
    for half in range(2):
        tall = jnp.concatenate([spectrum[:, k * N : (k + 1) * N] for k in range(4 * half, 4 * half + 4)], axis=0)
        send1[:, 0, half * N : (half + 1) * N] = tall.T
    lane = iota((N, N), 1)
    limits = jnp.where(lane < 64, limit_ref[0, 0], limit_ref[0, 1])
    send1[:, 0, 2 * N : 3 * N] = jnp.where((lane & 15) == b, limits, 0).astype(f32)

    def exchange(src, dst, s):
        for step in STEPS:
            t, dev = place(step)
            pltpu.make_async_remote_copy(src.at[t], dst.at[me], send_sems.at[s], recv_sems.at[s], device_id=dev, device_id_type=MESH).start()
        dst[me] = src[me]

    def arrived(src, dst, s):
        view = dst.at[pl.ds(0, N - 1)]
        pltpu.make_async_copy(view, view, recv_sems.at[s]).wait()

    pl.semaphore_wait(bar, N - 1)
    exchange(send1, recv1, 0)

    lanes = iota((1, 3 * 256), 1)
    proj = (lanes & 255) >> 4
    sines = jnp.zeros((1, 3 * 256), f32)
    for p in range(NPROJ):
        sines = jnp.where(proj == p, trig_ref[NANG + angle_ref[p]], sines)
    row_at = (16 * (lanes >> 8) - 16 + (lanes & 15)).astype(f32)
    tilt = (2.0 * iota((NZ, 1), 0).astype(f32) - (NZ - 1)) / (NZ - 1)
    away = row_at - (0.5 + (HALO - 1) * sines * tilt)
    for y in range(YB):
        rows_ref[y] = jnp.maximum(0.0, 1.0 - jnp.abs(away - 2.0 * y)).astype(bf16)
    fz = fold_freq(iota((NZ, 1), 0), NZ)
    fy = fold_freq(iota((1, NY), 1), NY)
    for k in range(KX):
        fx = fold_freq(me * KX + k + iota((1, NY), 1) * 0, NX)
        radius = fz + (fx + fy)
        low = (radius * (1.0 / (lower_edge * lower_edge))) ** 8
        up = (radius * (1.0 / (upper_edge * upper_edge))) ** 8
        gain_ref[:, k * NY : (k + 1) * NY] = low * (math.pi / NPROJ) / ((1.0 + low) * (1.0 + up))

    arrived(send1, recv1, 0)
    x = []
    for half in range(2):
        flat = recv1[:, 0, half * N : (half + 1) * N].T
        x += [flat[k * ROWS : (k + 1) * ROWS] for k in range(4)]
    group = iota((ROWS, N), 1) >> 4
    for bit in (1, 2, 4):
        clear = (group & bit) == 0
        for k in range(KX):
            if k & bit == 0:
                a, c = x[k], x[k + bit]
                x[k] = jnp.where(clear, a, pltpu.roll(c, 16 * bit, 1))
                x[k + bit] = jnp.where(clear, pltpu.roll(a, N - 16 * bit, 1), c)
    data = jnp.concatenate(x, axis=0)
    lims = jnp.sum(recv1[0:BANDS, 0, 2 * N : 3 * N], axis=0, keepdims=True)
    lane1 = iota((1, N), 1)
    swapped = pltpu.roll(lims, 64, 1)
    lo = jnp.where(lane1 < 64, lims, swapped)
    hi = jnp.where(lane1 < 64, swapped, lims)
    pieces = []
    for s in (-1, 0, 1):
        row = (16 * ((iota((RB, N), 1) & 15) + s) + iota((RB, N), 0)).astype(f32)
        ok = (row >= lo) & (row < hi) & (row >= 0.0) & (row < 256.0)
        keep = jnp.where(ok, 1.0, 0.0)
        moved = data if s == 0 else pltpu.roll(data, (-s) % N, 1)
        pieces += [(moved[r * RB : (r + 1) * RB] * keep).astype(bf16) for r in range(NPROJ)]
    extended = jnp.concatenate(pieces, axis=0)
    for y in range(YB):
        vol_ref[:, y * N : (y + 1) * N] = dot(rows_ref[y], extended).astype(bf16)
    loads[6].wait()
    loads[7].wait()
    along_y = dot(vol_ref[...], bands_ref[...]).astype(bf16)
    along_z = dot(small_ref[0], along_y) * gain_ref[...]
    along_z = along_z.astype(bf16)
    inverse_y = [dot(along_z[:, k * NY : (k + 1) * NY], small_ref[2]).astype(bf16) for k in range(KX)]
    back_ref[...] = dot(small_ref[1], jnp.concatenate(inverse_y, axis=1))
    for chunk in CHUNKS:
        first = pl.multiple_of(place2(chunk[0])[1][0] * BANDS, BANDS)
        for k in range(KX):
            mix_ref[pl.ds(first, BANDS), k, :] = back_ref[pl.ds(first, BANDS), k * NY : (k + 1) * NY]
        send2[pl.ds(first, BANDS)] = mix_ref[pl.ds(first, BANDS)].astype(bf16)
        for step in chunk:
            if any(step):
                t, dev = place2(step)
                pltpu.make_async_remote_copy(send2.at[t], recv2.at[me], send_sems.at[1], recv_sems.at[1], device_id=dev, device_id_type=MESH).start()
    recv2[me] = send2[me]
    arrived(send2, recv2, 1)
    for s, src in enumerate((send1, send2)):
        view = src.at[pl.ds(0, N - 1)]
        pltpu.make_async_copy(view, view, send_sems.at[s]).wait()


def on_device(projections, angle_index, row_ranges):
    ramp, forward, bands, inverse, small, trig = tables()
    vmem = pl.BlockSpec(memory_space=pltpu.VMEM)
    hbm = pl.BlockSpec(memory_space=pl.ANY)
    back = pl.pallas_call(
        kernel,
        name="laminograph",
        out_shape=jax.ShapeDtypeStruct((N, KX, NY), bf16),
        in_specs=[hbm] * 8,
        out_specs=vmem,
        scratch_shapes=[
            pltpu.SMEM((NPROJ,), jnp.int32),
            pltpu.SMEM((1, 2), jnp.int32),
            pltpu.SMEM(trig.shape, f32),
            pltpu.VMEM((ROWS, NU), bf16),
            pltpu.VMEM(ramp.shape, bf16),
            pltpu.VMEM(forward.shape, bf16),
            pltpu.VMEM(bands.shape, bf16),
            pltpu.VMEM(small.shape, bf16),
            pltpu.VMEM((NU // TILE * ROWS, TILE), bf16),
            pltpu.VMEM((ROWS, NU), bf16),
            pltpu.VMEM((ROWS, NX), f32),
            pltpu.VMEM((N, 1, 3 * N), f32),
            pltpu.VMEM((N, 1, 3 * N), f32),
            pltpu.VMEM((YB, NZ, 3 * 256), bf16),
            pltpu.VMEM((NZ, KX * NY), f32),
            pltpu.VMEM((NZ, YB * N), bf16),
            pltpu.VMEM((NZ, KX * NY), f32),
            pltpu.VMEM((NZ, KX, NY), f32),
            pltpu.VMEM((N, KX, NY), bf16),
            pltpu.SemaphoreType.DMA((8,)),
            pltpu.SemaphoreType.DMA((2,)),
            pltpu.SemaphoreType.DMA((2,)),
        ],
        compiler_params=pltpu.CompilerParams(collective_id=1, has_side_effects=True, vmem_limit_bytes=56 * 2**20),
    )(angle_index, row_ranges, trig, projections.reshape(ROWS, NU), ramp, forward, bands, small)
    return lax.dot_general(back.reshape(NX, NY), inverse, (((0,), (0,)), ((), ())), preferred_element_type=f32)[None]


def solution(mesh):
    return jax.shard_map(
        on_device,
        mesh=mesh,
        in_specs=(P("depth", "yband", None), P(), P("yband", None)),
        out_specs=P(("depth", "yband"), None, None),
        check_vma=False,
    )
```

```python
import math

import jax
import jax.numpy as jnp
import numpy as np
from jax import lax
from jax.experimental import pallas as pl
from jax.experimental.pallas import tpu as pltpu
from jax.sharding import PartitionSpec as P

NX, NU, NANG, NY, NZ = 1024, 2048, 1440, 128, 128
NP_DEV, YB, RB, HALO, BANDS, NPROJ = 2, 8, 16, 12, 16, 16
N = 128
KX = NX // N
ROWS = NP_DEV * RB
TILE = 256
WIN = 384
MESH = pl.DeviceIdType.MESH
lower_edge, upper_edge = 0.04, 0.35
f32, bf16 = jnp.float32, jnp.bfloat16


def far_first():
    steps = [(x, y, z, c) for x in range(4) for y in range(4) for z in range(4) for c in range(2)]
    hops = lambda s: sum(min(q, 4 - q) for q in s[:3])
    return sorted(steps, key=lambda s: (-hops(s), s))[:-2] + [(0, 0, 0, 1)]


def far_chunks():
    chunks = []
    for high, y in sorted([(h, y) for h in range(2) for y in range(4)], key=lambda q: (-2 * q[0] - min(q[1], 4 - q[1]), q)):
        inner = [(low, z, c) for low in range(2) for z in range(4) for c in range(2)]
        inner.sort(key=lambda q: (-abs(2 * high - q[0]) - min(q[1], 4 - q[1]), q))
        chunks.append([(high, low, y, z, c) for low, z, c in inner])
    return chunks


STEPS = far_first()
CHUNKS = far_chunks()


def real_basis(n):
    rows = np.arange(n)
    k = np.where(rows <= n // 2, rows, rows - n // 2)
    phase = 2.0 * np.pi * ((k[:, None] * rows[None, :]) % n) / n
    q = np.where((rows <= n // 2)[:, None], np.cos(phase), np.sin(phase))
    norm = np.where((rows == 0) | (rows == n // 2), 1.0 / n, 2.0 / n)
    return q * np.sqrt(norm)[:, None]


def ramp_tiles():
    n = np.arange(-(NU - 1), NU)
    odd = n % 2 != 0
    dist = np.where(odd, n, 1).astype(np.float32)
    values = np.where(n == 0, np.float32(0.25), np.where(odd, np.float32(-1.0) / (np.float32(math.pi * math.pi) * dist * dist), np.float32(0)))
    values = (values / np.float32(NX / NU)).astype(bf16)
    blocks = NU // TILE
    off = np.arange(1 - blocks, blocks)[:, None, None] * TILE
    at = off + np.arange(TILE)[None, :, None] - np.arange(TILE)[None, None, :]
    return values[at + NU - 1]


def tables():
    qx, qy, qz = real_basis(NX), real_basis(NY), real_basis(NZ)
    order = (np.arange(N)[None, :] * KX + np.arange(KX)[:, None]).reshape(-1)
    forward_x = qx.T[:, order]
    by_band = qy.reshape(NY, BANDS, YB).transpose(0, 2, 1).reshape(NY, NY)
    small = np.stack([qz.T, by_band, qy.T])
    angle = (np.float32(2.0 * math.pi) * np.arange(NANG, dtype=np.float32) / np.float32(NANG)).astype(np.float64)
    trig = np.concatenate([np.cos(angle), np.sin(angle)]).astype(np.float32)
    return (
        jnp.asarray(ramp_tiles()),
        jnp.asarray(forward_x.astype(np.float32), bf16),
        jnp.asarray(qx.astype(np.float32), bf16),
        jnp.asarray(small.astype(np.float32), bf16),
        jnp.asarray(trig),
    )


def iota(shape, axis):
    return lax.broadcasted_iota(jnp.int32, shape, axis)


def dot(a, b):
    return jnp.dot(a, b, preferred_element_type=f32)


def fold_freq(row, n):
    k = jnp.where(row <= n // 2, row, row - n // 2).astype(f32) / n
    return k * k


def kernel(
    angle_hbm, limit_hbm, trig_hbm, proj_hbm, ramp_hbm, forward_hbm, small_hbm,
    recv2,
    angle_ref, limit_ref, trig_ref, proj_ref, ramp_ref, forward_ref, small_ref,
    stack_ref, filt_ref, g_ref, send1, recv1, rows_ref, gain_ref, back_ref, mix_ref, send2,
    table_sems, send_sems, recv_sems,
):
    d = lax.axis_index("depth")
    b = lax.axis_index("yband")
    me = d * BANDS + b

    px, py = ((d >> 2) << 1) | (b >> 3), d & 3
    pz, pc = (b >> 1) & 3, b & 1

    def place(step):
        dx, dy, dz, dc = step
        x, y, z, c = (px + dx) & 3, (py + dy) & 3, (pz + dz) & 3, pc ^ dc
        dd, bb = ((x >> 1) << 2) | y, ((x & 1) << 3) | (z << 1) | c
        return dd * BANDS + bb, (dd, bb)

    def place2(step):
        high, low, y, z, c = step
        dd = (((d >> 2) ^ high) << 2) | ((py + y) & 3)
        bb = (((b >> 3) ^ low) << 3) | (((pz + z) & 3) << 1) | (pc ^ c)
        return dd * BANDS + bb, (dd, bb)

    pairs = [(proj_hbm, proj_ref), (ramp_hbm, ramp_ref), (angle_hbm, angle_ref), (trig_hbm, trig_ref), (limit_hbm, limit_ref)]
    pairs += [(forward_hbm, forward_ref), (small_hbm, small_ref)]
    loads = [pltpu.make_async_copy(src, dst, table_sems.at[i]) for i, (src, dst) in enumerate(pairs)]
    for i in (0, 1, 5):
        loads[i].start()

    bar = pltpu.get_barrier_semaphore()

    for step in STEPS:
        pl.semaphore_signal(bar, inc=1, device_id=place(step)[1], device_id_type=MESH)

    for i in (2, 3, 4, 6):
        loads[i].start()

    blocks = NU // TILE
    loads[0].wait()
    for i in range(blocks):
        stack_ref[i * ROWS : (i + 1) * ROWS, :] = proj_ref[:, i * TILE : (i + 1) * TILE]
    loads[1].wait()
    acc = [jnp.zeros((ROWS, TILE), f32) for _ in range(blocks)]
    for k in range(1 - blocks, blocks):
        first, last = max(k, 0), blocks + min(k, 0)
        part = dot(stack_ref[first * ROWS : last * ROWS, :], ramp_ref[k + blocks - 1])
        for i in range(first, last):
            acc[i - k] += part[(i - first) * ROWS : (i - first + 1) * ROWS]
    for j in range(blocks):
        filt_ref[:, j * TILE : (j + 1) * TILE] = acc[j].astype(bf16)

    for load in loads[2:5]:
        load.wait()
    sub = iota((WIN, N), 0).astype(f32)
    lane_x = iota((1, N), 1).astype(f32)
    for p in range(NP_DEV):
        slope = jnp.full((1, N), 2.0 * trig_ref[angle_ref[d * NP_DEV + p]])
        rows = [filt_ref[p * RB : (p + 1) * RB, i * N : (i + 1) * N] for i in range(NU // N)]
        for i in range(NX // N):
            column = (NU - 1) / 2.0 + slope * ((lane_x + float(i * N)) - (NX - 1) / 2.0)
            ends = [(NU - 1) / 2.0 + slope * (i * N + end - (NX - 1) / 2.0) for end in (0.0, N - 1.0)]
            tile = jnp.clip(jnp.floor(jnp.minimum(ends[0], ends[1]) * (1.0 / N)), 0.0, float((NU - WIN) // N))
            column = column - tile * float(N)
            weights = jnp.maximum(0.0, 1.0 - jnp.abs(sub - column)).astype(bf16)
            window = rows
            for bit in (8, 4, 2, 1):
                up = tile >= float(bit)
                tile = jnp.where(up, tile - float(bit), tile)
                upper = jnp.broadcast_to(up, (RB, N))
                keep = bit - 1 + WIN // N
                window = [jnp.where(upper, window[k + bit], window[k]) if k + bit < len(window) else window[k] for k in range(keep)]
            g_ref[p * RB : (p + 1) * RB, i * N : (i + 1) * N] = dot(jnp.concatenate(window, axis=1), weights)

    g = g_ref[...]
    g_high = g.astype(bf16)
    g_low = (g - g_high.astype(f32)).astype(bf16)
    loads[5].wait()
    both = dot(jnp.concatenate([g_high, g_low], axis=0), forward_ref[...])
    spectrum = both[:ROWS] + both[ROWS:]
    for half in range(2):
        tall = jnp.concatenate([spectrum[:, k * N : (k + 1) * N] for k in range(4 * half, 4 * half + 4)], axis=0)
        send1[:, 0, half * N : (half + 1) * N] = tall.T
    lane = iota((N, N), 1)
    limits = jnp.where(lane < 64, limit_ref[0, 0], limit_ref[0, 1])
    send1[:, 0, 2 * N : 3 * N] = limits.astype(f32)

    def exchange(src, dst, s):
        for step in STEPS:
            t, dev = place(step)
            pltpu.make_async_remote_copy(src.at[t], dst.at[me], send_sems.at[s], recv_sems.at[s], device_id=dev, device_id_type=MESH).start()
        dst[me] = src[me]

    def arrived(src, dst, s):
        view = dst.at[pl.ds(0, N - 1)]
        pltpu.make_async_copy(view, view, recv_sems.at[s]).wait()

    pl.semaphore_wait(bar, N - 1)
    exchange(send1, recv1, 0)

    loads[6].wait()
    detector = iota((RB, NZ), 0).astype(f32)
    tilt = (2.0 * iota((1, NZ), 1).astype(f32) - (NZ - 1)) / (NZ - 1)
    offsets = [0.5 + (HALO - 1) * trig_ref[NANG + angle_ref[p]] * tilt for p in range(NPROJ)]
    away = jnp.concatenate([detector + 16.0 * s - offsets[p] for s in (-1, 0, 1) for p in range(NPROJ)], axis=0)
    for y in range(YB):
        weights = jnp.maximum(0.0, 1.0 - jnp.abs(away - 2.0 * y)).astype(bf16)
        rows_ref[:, y * NZ : (y + 1) * NZ] = dot(weights, small_ref[0]).astype(bf16)
    fy = fold_freq(iota((NY, 1), 0), NY)
    fz = fold_freq(iota((1, NZ), 1), NZ)
    for k in range(KX):
        fx = fold_freq(me * KX + k + iota((1, NZ), 1) * 0, NX)
        radius = fy + (fx + fz)
        low = (radius * (1.0 / (lower_edge * lower_edge))) ** 8
        up = (radius * (1.0 / (upper_edge * upper_edge))) ** 8
        gain_ref[:, k * NZ : (k + 1) * NZ] = low * (math.pi / NPROJ) / ((1.0 + low) * (1.0 + up))

    arrived(send1, recv1, 0)
    group = iota((BANDS, N), 1) >> 5
    field = [[None, None] for _ in range(KX)]
    for half in range(2):
        for j in range(2):
            x = [recv1[(4 * j + q) * BANDS : (4 * j + q + 1) * BANDS, 0, half * N : (half + 1) * N] for q in range(4)]
            for bit in (1, 2):
                clear = (group & bit) == 0
                for q in range(4):
                    if q & bit == 0:
                        a, c = x[q], x[q + bit]
                        x[q] = jnp.where(clear, a, pltpu.roll(c, 32 * bit, 1))
                        x[q + bit] = jnp.where(clear, pltpu.roll(a, N - 32 * bit, 1), c)
            for q in range(4):
                field[4 * half + q][j] = x[q]
    lims = recv1[0:BANDS, 0, 2 * N : 3 * N]
    swapped = pltpu.roll(lims, 64, 1)
    left = iota((BANDS, N), 1) < 64
    lo, hi = jnp.where(left, lims, swapped), jnp.where(left, swapped, lims)
    columns = []
    for s in (-1, 0, 1):
        row = (16 * (iota((BANDS, N), 0) + s) + (iota((BANDS, N), 1) & 15)).astype(f32)
        ok = (row >= lo) & (row < hi) & (row >= 0.0) & (row < 256.0)
        keep = jnp.where(ok, 1.0, 0.0)
        for j in range(2):
            moved = [field[k][j] if s == 0 else pltpu.roll(field[k][j], (-s) % BANDS, 0) for k in range(KX)]
            columns.append(jnp.concatenate([(m * keep).astype(bf16) for m in moved], axis=0))
    vol = dot(jnp.concatenate(columns, axis=1), rows_ref[...]).astype(bf16)
    tall = [
        jnp.concatenate([vol[k * BANDS : (k + 1) * BANDS, y * NZ : (y + 1) * NZ] for y in range(YB)], axis=0)
        for k in range(KX)
    ]
    along_y = dot(small_ref[1], jnp.concatenate(tall, axis=1))
    back_y = dot(small_ref[2], (along_y * gain_ref[...]).astype(bf16)).astype(bf16)
    for k in range(KX):
        back_ref[:, k * NY : (k + 1) * NY] = lax.dot_general(
            small_ref[0], back_y[:, k * NZ : (k + 1) * NZ], (((1,), (1,)), ((), ())), preferred_element_type=f32
        )
    for chunk in CHUNKS:
        first = pl.multiple_of(place2(chunk[0])[1][0] * BANDS, BANDS)
        for k in range(KX):
            mix_ref[pl.ds(first, BANDS), k, :] = back_ref[pl.ds(first, BANDS), k * NY : (k + 1) * NY]
        send2[pl.ds(first, BANDS)] = mix_ref[pl.ds(first, BANDS)].astype(bf16)
        for step in chunk:
            if any(step):
                t, dev = place2(step)
                pltpu.make_async_remote_copy(send2.at[t], recv2.at[me], send_sems.at[1], recv_sems.at[1], device_id=dev, device_id_type=MESH).start()
    recv2[me] = send2[me]
    arrived(send2, recv2, 1)
    for s, src in enumerate((send1, send2)):
        view = src.at[pl.ds(0, N - 1)]
        pltpu.make_async_copy(view, view, send_sems.at[s]).wait()


def on_device(projections, angle_index, row_ranges):
    ramp, forward, inverse, small, trig = tables()
    vmem = pl.BlockSpec(memory_space=pltpu.VMEM)
    hbm = pl.BlockSpec(memory_space=pl.ANY)
    back = pl.pallas_call(
        kernel,
        name="laminograph",
        out_shape=jax.ShapeDtypeStruct((N, KX, NY), bf16),
        in_specs=[hbm] * 7,
        out_specs=vmem,
        scratch_shapes=[
            pltpu.SMEM((NPROJ,), jnp.int32),
            pltpu.SMEM((1, 2), jnp.int32),
            pltpu.SMEM(trig.shape, f32),
            pltpu.VMEM((ROWS, NU), bf16),
            pltpu.VMEM(ramp.shape, bf16),
            pltpu.VMEM(forward.shape, bf16),
            pltpu.VMEM(small.shape, bf16),
            pltpu.VMEM((NU // TILE * ROWS, TILE), bf16),
            pltpu.VMEM((ROWS, NU), bf16),
            pltpu.VMEM((ROWS, NX), f32),
            pltpu.VMEM((N, 1, 3 * N), f32),
            pltpu.VMEM((N, 1, 3 * N), f32),
            pltpu.VMEM((3 * 256, YB * NZ), bf16),
            pltpu.VMEM((NZ, KX * NY), f32),
            pltpu.VMEM((NZ, KX * NY), f32),
            pltpu.VMEM((NZ, KX, NY), f32),
            pltpu.VMEM((N, KX, NY), bf16),
            pltpu.SemaphoreType.DMA((7,)),
            pltpu.SemaphoreType.DMA((2,)),
            pltpu.SemaphoreType.DMA((2,)),
        ],
        compiler_params=pltpu.CompilerParams(collective_id=1, has_side_effects=True, vmem_limit_bytes=56 * 2**20),
    )(angle_index, row_ranges, trig, projections.reshape(ROWS, NU), ramp, forward, small)
    return lax.dot_general(back.reshape(NX, NY), inverse, (((0,), (0,)), ((), ())), preferred_element_type=f32)[None]


def solution(mesh):
    return jax.shard_map(
        on_device,
        mesh=mesh,
        in_specs=(P("depth", "yband", None), P(), P("yband", None)),
        out_specs=P(("depth", "yband"), None, None),
        check_vma=False,
    )
```

```python
import math

import jax
import jax.numpy as jnp
import numpy as np
from jax import lax
from jax.experimental import pallas as pl
from jax.experimental.pallas import tpu as pltpu
from jax.sharding import PartitionSpec as P

NX, NU, NANG, NY, NZ = 1024, 2048, 1440, 128, 128
NP_DEV, YB, RB, HALO, BANDS, NPROJ = 2, 8, 16, 12, 16, 16
N = 128
KX = NX // N
ROWS = NP_DEV * RB
TILE = 256
WIN = 384
MESH = pl.DeviceIdType.MESH
lower_edge, upper_edge = 0.04, 0.35
f32, bf16 = jnp.float32, jnp.bfloat16


def far_first():
    steps = [(x, y, z, c) for x in range(4) for y in range(4) for z in range(4) for c in range(2)]
    hops = lambda s: sum(min(q, 4 - q) for q in s[:3])
    return sorted(steps, key=lambda s: (-hops(s), s))[:-2] + [(0, 0, 0, 1)]


def far_chunks():
    chunks = []
    for high, y in sorted([(h, y) for h in range(2) for y in range(4)], key=lambda q: (-2 * q[0] - min(q[1], 4 - q[1]), q)):
        inner = [(low, z, c) for low in range(2) for z in range(4) for c in range(2)]
        inner.sort(key=lambda q: (-abs(2 * high - q[0]) - min(q[1], 4 - q[1]), q))
        chunks.append([(high, low, y, z, c) for low, z, c in inner])
    return chunks


STEPS = far_first()
CHUNKS = far_chunks()


def real_basis(n):
    rows = np.arange(n)
    k = np.where(rows <= n // 2, rows, rows - n // 2)
    phase = 2.0 * np.pi * ((k[:, None] * rows[None, :]) % n) / n
    q = np.where((rows <= n // 2)[:, None], np.cos(phase), np.sin(phase))
    norm = np.where((rows == 0) | (rows == n // 2), 1.0 / n, 2.0 / n)
    return q * np.sqrt(norm)[:, None]


def ramp_tiles():
    n = np.arange(-(NU - 1), NU)
    odd = n % 2 != 0
    dist = np.where(odd, n, 1).astype(np.float32)
    values = np.where(n == 0, np.float32(0.25), np.where(odd, np.float32(-1.0) / (np.float32(math.pi * math.pi) * dist * dist), np.float32(0)))
    values = (values / np.float32(NX / NU)).astype(bf16)
    blocks = NU // TILE
    off = np.arange(1 - blocks, blocks)[:, None, None] * TILE
    at = off + np.arange(TILE)[None, :, None] - np.arange(TILE)[None, None, :]
    return values[at + NU - 1]


def tables():
    qx, qy, qz = real_basis(NX), real_basis(NY), real_basis(NZ)
    order = (np.arange(N)[None, :] * KX + np.arange(KX)[:, None]).reshape(-1)
    forward_x = qx.T[:, order]
    by_band = qy.reshape(NY, BANDS, YB).transpose(0, 2, 1).reshape(NY, NY)
    small = np.stack([qz.T, by_band, qy.T])
    angle = (np.float32(2.0 * math.pi) * np.arange(NANG, dtype=np.float32) / np.float32(NANG)).astype(np.float64)
    trig = np.concatenate([np.cos(angle), np.sin(angle)]).astype(np.float32)
    return (
        jnp.asarray(ramp_tiles()),
        jnp.asarray(forward_x.astype(np.float32), bf16),
        jnp.asarray(qx.astype(np.float32), bf16),
        jnp.asarray(small.astype(np.float32), bf16),
        jnp.asarray(trig),
    )


def iota(shape, axis):
    return lax.broadcasted_iota(jnp.int32, shape, axis)


def dot(a, b):
    return jnp.dot(a, b, preferred_element_type=f32)


def fold_freq(row, n):
    k = jnp.where(row <= n // 2, row, row - n // 2).astype(f32) / n
    return k * k


def kernel(
    angle_hbm, limit_hbm, trig_hbm, proj_hbm, ramp_hbm, forward_hbm, small_hbm,
    recv2,
    angle_ref, limit_ref, trig_ref, proj_ref, ramp_ref, forward_ref, small_ref,
    stack_ref, filt_ref, g_ref, send1, recv1, rows_ref, gain_ref, back_ref, mix_ref, send2,
    table_sems, send_sems, recv_sems,
):
    d = lax.axis_index("depth")
    b = lax.axis_index("yband")
    me = d * BANDS + b

    px, py = ((d >> 2) << 1) | (b >> 3), d & 3
    pz, pc = (b >> 1) & 3, b & 1

    def place(step):
        dx, dy, dz, dc = step
        x, y, z, c = (px + dx) & 3, (py + dy) & 3, (pz + dz) & 3, pc ^ dc
        dd, bb = ((x >> 1) << 2) | y, ((x & 1) << 3) | (z << 1) | c
        return dd * BANDS + bb, (dd, bb)

    def place2(step):
        high, low, y, z, c = step
        dd = (((d >> 2) ^ high) << 2) | ((py + y) & 3)
        bb = (((b >> 3) ^ low) << 3) | (((pz + z) & 3) << 1) | (pc ^ c)
        return dd * BANDS + bb, (dd, bb)

    pairs = [(proj_hbm, proj_ref), (ramp_hbm, ramp_ref), (angle_hbm, angle_ref), (trig_hbm, trig_ref), (limit_hbm, limit_ref)]
    pairs += [(forward_hbm, forward_ref), (small_hbm, small_ref)]
    loads = [pltpu.make_async_copy(src, dst, table_sems.at[i]) for i, (src, dst) in enumerate(pairs)]
    for i in (0, 1, 5):
        loads[i].start()

    bar = pltpu.get_barrier_semaphore()

    for step in STEPS:
        pl.semaphore_signal(bar, inc=1, device_id=place(step)[1], device_id_type=MESH)

    for i in (2, 3, 4, 6):
        loads[i].start()

    blocks = NU // TILE
    loads[0].wait()
    for i in range(blocks):
        stack_ref[i * ROWS : (i + 1) * ROWS, :] = proj_ref[:, i * TILE : (i + 1) * TILE]
    loads[1].wait()
    acc = [jnp.zeros((ROWS, TILE), f32) for _ in range(blocks)]
    for k in range(1 - blocks, blocks):
        first, last = max(k, 0), blocks + min(k, 0)
        part = dot(stack_ref[first * ROWS : last * ROWS, :], ramp_ref[k + blocks - 1])
        for i in range(first, last):
            acc[i - k] += part[(i - first) * ROWS : (i - first + 1) * ROWS]
    for j in range(blocks):
        filt_ref[:, j * TILE : (j + 1) * TILE] = acc[j].astype(bf16)

    for load in loads[2:5]:
        load.wait()
    sub = iota((WIN, N), 0).astype(f32)
    lane_x = iota((1, N), 1).astype(f32)
    for p in range(NP_DEV):
        slope = jnp.full((1, N), 2.0 * trig_ref[angle_ref[d * NP_DEV + p]])
        rows = [filt_ref[p * RB : (p + 1) * RB, i * N : (i + 1) * N] for i in range(NU // N)]
        for i in range(NX // N):
            column = (NU - 1) / 2.0 + slope * ((lane_x + float(i * N)) - (NX - 1) / 2.0)
            ends = [(NU - 1) / 2.0 + slope * (i * N + end - (NX - 1) / 2.0) for end in (0.0, N - 1.0)]
            tile = jnp.clip(jnp.floor(jnp.minimum(ends[0], ends[1]) * (1.0 / N)), 0.0, float((NU - WIN) // N))
            column = column - tile * float(N)
            weights = jnp.maximum(0.0, 1.0 - jnp.abs(sub - column)).astype(bf16)
            window = rows
            for bit in (8, 4, 2, 1):
                up = tile >= float(bit)
                tile = jnp.where(up, tile - float(bit), tile)
                upper = jnp.broadcast_to(up, (RB, N))
                keep = bit - 1 + WIN // N
                window = [jnp.where(upper, window[k + bit], window[k]) if k + bit < len(window) else window[k] for k in range(keep)]
            g_ref[p * RB : (p + 1) * RB, i * N : (i + 1) * N] = dot(jnp.concatenate(window, axis=1), weights)

    g = g_ref[...]
    g_high = g.astype(bf16)
    g_low = (g - g_high.astype(f32)).astype(bf16)
    loads[5].wait()
    both = dot(jnp.concatenate([g_high, g_low], axis=0), forward_ref[...])
    spectrum = both[:ROWS] + both[ROWS:]
    for half in range(2):
        tall = jnp.concatenate([spectrum[:, k * N : (k + 1) * N] for k in range(4 * half, 4 * half + 4)], axis=0)
        send1[:, 0, half * N : (half + 1) * N] = tall.T
    lane = iota((N, N), 1)
    limits = jnp.where(lane < 64, limit_ref[0, 0], limit_ref[0, 1])
    send1[:, 0, 2 * N : 3 * N] = limits.astype(f32)

    def exchange(src, dst, s):
        for step in STEPS:
            t, dev = place(step)
            pltpu.make_async_remote_copy(src.at[t], dst.at[me], send_sems.at[s], recv_sems.at[s], device_id=dev, device_id_type=MESH).start()
        dst[me] = src[me]

    def arrived(src, dst, s):
        view = dst.at[pl.ds(0, N - 1)]
        pltpu.make_async_copy(view, view, recv_sems.at[s]).wait()

    pl.semaphore_wait(bar, N - 1)
    exchange(send1, recv1, 0)

    loads[6].wait()
    detector = iota((RB, NZ), 0).astype(f32)
    tilt = (2.0 * iota((1, NZ), 1).astype(f32) - (NZ - 1)) / (NZ - 1)
    offsets = [0.5 + (HALO - 1) * trig_ref[NANG + angle_ref[p]] * tilt for p in range(NPROJ)]
    away = jnp.concatenate([detector + 16.0 * s - offsets[p] for s in (-1, 0, 1) for p in range(NPROJ)], axis=0)
    for y in range(YB):
        weights = jnp.maximum(0.0, 1.0 - jnp.abs(away - 2.0 * y)).astype(bf16)
        rows_ref[:, y * NZ : (y + 1) * NZ] = dot(weights, small_ref[0]).astype(bf16)
    fy = fold_freq(iota((NY, 1), 0), NY)
    fz = fold_freq(iota((1, NZ), 1), NZ)
    for k in range(KX):
        fx = fold_freq(me * KX + k + iota((1, NZ), 1) * 0, NX)
        radius = fy + (fx + fz)
        low = (radius * (1.0 / (lower_edge * lower_edge))) ** 8
        up = (radius * (1.0 / (upper_edge * upper_edge))) ** 8
        gain_ref[:, k * NZ : (k + 1) * NZ] = low * (math.pi / NPROJ) / ((1.0 + low) * (1.0 + up))

    arrived(send1, recv1, 0)
    group = iota((BANDS, N), 1) >> 5
    field = [[None, None] for _ in range(KX)]
    for half in range(2):
        for j in range(2):
            x = [recv1[(4 * j + q) * BANDS : (4 * j + q + 1) * BANDS, 0, half * N : (half + 1) * N] for q in range(4)]
            for bit in (1, 2):
                clear = (group & bit) == 0
                for q in range(4):
                    if q & bit == 0:
                        a, c = x[q], x[q + bit]
                        x[q] = jnp.where(clear, a, pltpu.roll(c, 32 * bit, 1))
                        x[q + bit] = jnp.where(clear, pltpu.roll(a, N - 32 * bit, 1), c)
            for q in range(4):
                field[4 * half + q][j] = x[q]
    lims = recv1[0:BANDS, 0, 2 * N : 3 * N]
    swapped = pltpu.roll(lims, 64, 1)
    left = iota((BANDS, N), 1) < 64
    lo, hi = jnp.where(left, lims, swapped), jnp.where(left, swapped, lims)
    columns = []
    for s in (-1, 0, 1):
        row = (16 * (iota((BANDS, N), 0) + s) + (iota((BANDS, N), 1) & 15)).astype(f32)
        ok = (row >= lo) & (row < hi) & (row >= 0.0) & (row < 256.0)
        keep = jnp.where(ok, 1.0, 0.0)
        for j in range(2):
            moved = [field[k][j] if s == 0 else pltpu.roll(field[k][j], (-s) % BANDS, 0) for k in range(KX)]
            columns.append(jnp.concatenate([(m * keep).astype(bf16) for m in moved], axis=0))
    vol = dot(jnp.concatenate(columns, axis=1), rows_ref[...]).astype(bf16)
    tall = [
        jnp.concatenate([vol[k * BANDS : (k + 1) * BANDS, y * NZ : (y + 1) * NZ] for y in range(YB)], axis=0)
        for k in range(KX)
    ]
    along_y = dot(small_ref[1], jnp.concatenate(tall, axis=1))
    back_y = dot(small_ref[2], (along_y * gain_ref[...]).astype(bf16)).astype(bf16)
    for k in range(KX):
        back_ref[:, k * NY : (k + 1) * NY] = lax.dot_general(
            small_ref[0], back_y[:, k * NZ : (k + 1) * NZ], (((1,), (1,)), ((), ())), preferred_element_type=f32
        )
    for chunk in CHUNKS:
        first = pl.multiple_of(place2(chunk[0])[1][0] * BANDS, BANDS)
        for k in range(KX):
            mix_ref[pl.ds(first, BANDS), k, :] = back_ref[pl.ds(first, BANDS), k * NY : (k + 1) * NY]
        send2[pl.ds(first, BANDS)] = mix_ref[pl.ds(first, BANDS)].astype(bf16)
        for step in chunk:
            if any(step):
                t, dev = place2(step)
                pltpu.make_async_remote_copy(send2.at[t], recv2.at[me], send_sems.at[1], recv_sems.at[1], device_id=dev, device_id_type=MESH).start()
    recv2[me] = send2[me]
    arrived(send2, recv2, 1)
    for s, src in enumerate((send1, send2)):
        view = src.at[pl.ds(0, N - 1)]
        pltpu.make_async_copy(view, view, send_sems.at[s]).wait()


def on_device(projections, angle_index, row_ranges):
    ramp, forward, inverse, small, trig = tables()
    vmem = pl.BlockSpec(memory_space=pltpu.VMEM)
    hbm = pl.BlockSpec(memory_space=pl.ANY)
    back = pl.pallas_call(
        kernel,
        name="laminograph",
        out_shape=jax.ShapeDtypeStruct((N, KX, NY), bf16),
        in_specs=[hbm] * 7,
        out_specs=vmem,
        scratch_shapes=[
            pltpu.SMEM((NPROJ,), jnp.int32),
            pltpu.SMEM((1, 2), jnp.int32),
            pltpu.SMEM(trig.shape, f32),
            pltpu.VMEM((ROWS, NU), bf16),
            pltpu.VMEM(ramp.shape, bf16),
            pltpu.VMEM(forward.shape, bf16),
            pltpu.VMEM(small.shape, bf16),
            pltpu.VMEM((NU // TILE * ROWS, TILE), bf16),
            pltpu.VMEM((ROWS, NU), bf16),
            pltpu.VMEM((ROWS, NX), f32),
            pltpu.VMEM((N, 1, 3 * N), f32),
            pltpu.VMEM((N, 1, 3 * N), f32),
            pltpu.VMEM((3 * 256, YB * NZ), bf16),
            pltpu.VMEM((NZ, KX * NY), f32),
            pltpu.VMEM((NZ, KX * NY), f32),
            pltpu.VMEM((NZ, KX, NY), f32),
            pltpu.VMEM((N, KX, NY), bf16),
            pltpu.SemaphoreType.DMA((7,)),
            pltpu.SemaphoreType.DMA((2,)),
            pltpu.SemaphoreType.DMA((2,)),
        ],
        compiler_params=pltpu.CompilerParams(collective_id=1, has_side_effects=True, vmem_limit_bytes=24 * 2**20),
    )(*[pltpu.with_memory_space_constraint(x, pltpu.HBM) for x in (angle_index, row_ranges, trig, projections.reshape(ROWS, NU), ramp, forward, small)])
    return lax.dot_general(back.reshape(NX, NY), inverse, (((0,), (0,)), ((), ())), preferred_element_type=f32)[None]


def solution(mesh):
    return jax.shard_map(
        on_device,
        mesh=mesh,
        in_specs=(P("depth", "yband", None), P(), P("yband", None)),
        out_specs=P(("depth", "yband"), None, None),
        check_vma=False,
    )
```

```python
import math

import jax
import jax.numpy as jnp
import numpy as np
from jax import lax
from jax.experimental import pallas as pl
from jax.experimental.pallas import tpu as pltpu
from jax.sharding import PartitionSpec as P

NX, NU, NANG, NY, NZ = 1024, 2048, 1440, 128, 128
NP_DEV, YB, RB, HALO, BANDS, NPROJ = 2, 8, 16, 12, 16, 16
N = 128
KX = NX // N
ROWS = NP_DEV * RB
TILE = 256
WIN = 384
MESH = pl.DeviceIdType.MESH
lower_edge, upper_edge = 0.04, 0.35
f32, bf16 = jnp.float32, jnp.bfloat16


def far_first():
    steps = [(x, y, z, c) for x in range(4) for y in range(4) for z in range(4) for c in range(2)]
    hops = lambda s: sum(min(q, 4 - q) for q in s[:3])
    return sorted(steps, key=lambda s: (-hops(s), s))[:-2] + [(0, 0, 0, 1)]


def far_chunks():
    chunks = []
    for high, y in sorted([(h, y) for h in range(2) for y in range(4)], key=lambda q: (-2 * q[0] - min(q[1], 4 - q[1]), q)):
        inner = [(low, z, c) for low in range(2) for z in range(4) for c in range(2)]
        inner.sort(key=lambda q: (-abs(2 * high - q[0]) - min(q[1], 4 - q[1]), q))
        chunks.append([(high, low, y, z, c) for low, z, c in inner])
    return chunks


STEPS = far_first()
CHUNKS = far_chunks()


def real_basis(n):
    rows = np.arange(n)
    k = np.where(rows <= n // 2, rows, rows - n // 2)
    phase = 2.0 * np.pi * ((k[:, None] * rows[None, :]) % n) / n
    q = np.where((rows <= n // 2)[:, None], np.cos(phase), np.sin(phase))
    norm = np.where((rows == 0) | (rows == n // 2), 1.0 / n, 2.0 / n)
    return q * np.sqrt(norm)[:, None]


def ramp_tiles():
    n = np.arange(-(NU - 1), NU)
    odd = n % 2 != 0
    dist = np.where(odd, n, 1).astype(np.float32)
    values = np.where(n == 0, np.float32(0.25), np.where(odd, np.float32(-1.0) / (np.float32(math.pi * math.pi) * dist * dist), np.float32(0)))
    values = (values / np.float32(NX / NU)).astype(bf16)
    blocks = NU // TILE
    off = np.arange(1 - blocks, blocks)[:, None, None] * TILE
    at = off + np.arange(TILE)[None, :, None] - np.arange(TILE)[None, None, :]
    return values[at + NU - 1]


def tables():
    qx, qy, qz = real_basis(NX), real_basis(NY), real_basis(NZ)
    order = (np.arange(N)[None, :] * KX + np.arange(KX)[:, None]).reshape(-1)
    forward_x = qx.T[:, order]
    by_band = qy.reshape(NY, BANDS, YB).transpose(0, 2, 1).reshape(NY, NY)
    small = np.stack([qz.T, by_band, qy.T])
    angle = (np.float32(2.0 * math.pi) * np.arange(NANG, dtype=np.float32) / np.float32(NANG)).astype(np.float64)
    trig = np.concatenate([np.cos(angle), np.sin(angle)]).astype(np.float32)
    return (
        jnp.asarray(ramp_tiles()),
        jnp.asarray(forward_x.astype(np.float32), bf16),
        jnp.asarray(qx.astype(np.float32), bf16),
        jnp.asarray(small.astype(np.float32), bf16),
        jnp.asarray(trig),
    )


def iota(shape, axis):
    return lax.broadcasted_iota(jnp.int32, shape, axis)


def dot(a, b):
    return jnp.dot(a, b, preferred_element_type=f32)


def fold_freq(row, n):
    k = jnp.where(row <= n // 2, row, row - n // 2).astype(f32) / n
    return k * k


def kernel(
    angle_hbm, limit_hbm, trig_hbm, proj_hbm, ramp_hbm, forward_hbm, small_hbm,
    recv2,
    angle_ref, limit_ref, trig_ref, proj_ref, ramp_ref, forward_ref, small_ref,
    stack_ref, filt_ref, g_ref, send1, recv1, rows_ref, gain_ref, back_ref, mix_ref, send2,
    limit_out, limit_in, table_sems, send_sems, recv_sems, limit_sems,
):
    d = lax.axis_index("depth")
    b = lax.axis_index("yband")
    me = d * BANDS + b

    px, py = ((d >> 2) << 1) | (b >> 3), d & 3
    pz, pc = (b >> 1) & 3, b & 1

    def place(step):
        dx, dy, dz, dc = step
        x, y, z, c = (px + dx) & 3, (py + dy) & 3, (pz + dz) & 3, pc ^ dc
        dd, bb = ((x >> 1) << 2) | y, ((x & 1) << 3) | (z << 1) | c
        return dd * BANDS + bb, (dd, bb)

    def place2(step):
        high, low, y, z, c = step
        dd = (((d >> 2) ^ high) << 2) | ((py + y) & 3)
        bb = (((b >> 3) ^ low) << 3) | (((pz + z) & 3) << 1) | (pc ^ c)
        return dd * BANDS + bb, (dd, bb)

    pairs = [(proj_hbm, proj_ref), (ramp_hbm, ramp_ref), (angle_hbm, angle_ref), (trig_hbm, trig_ref), (limit_hbm, limit_ref)]
    pairs += [(forward_hbm, forward_ref), (small_hbm, small_ref)]
    loads = [pltpu.make_async_copy(src, dst, table_sems.at[i]) for i, (src, dst) in enumerate(pairs)]
    for i in (0, 1, 5):
        loads[i].start()

    bar = pltpu.get_barrier_semaphore()

    for step in STEPS:
        pl.semaphore_signal(bar, inc=1, device_id=place(step)[1], device_id_type=MESH)

    for i in (2, 3, 4, 6):
        loads[i].start()

    blocks = NU // TILE
    loads[0].wait()
    for i in range(blocks):
        stack_ref[i * ROWS : (i + 1) * ROWS, :] = proj_ref[:, i * TILE : (i + 1) * TILE]
    loads[1].wait()
    acc = [jnp.zeros((ROWS, TILE), f32) for _ in range(blocks)]
    for k in range(1 - blocks, blocks):
        first, last = max(k, 0), blocks + min(k, 0)
        part = dot(stack_ref[first * ROWS : last * ROWS, :], ramp_ref[k + blocks - 1])
        for i in range(first, last):
            acc[i - k] += part[(i - first) * ROWS : (i - first + 1) * ROWS]
    for j in range(blocks):
        filt_ref[:, j * TILE : (j + 1) * TILE] = acc[j].astype(bf16)

    for load in loads[2:5]:
        load.wait()
    sub = iota((WIN, N), 0).astype(f32)
    lane_x = iota((1, N), 1).astype(f32)
    for p in range(NP_DEV):
        slope = jnp.full((1, N), 2.0 * trig_ref[angle_ref[d * NP_DEV + p]])
        rows = [filt_ref[p * RB : (p + 1) * RB, i * N : (i + 1) * N] for i in range(NU // N)]
        for i in range(NX // N):
            column = (NU - 1) / 2.0 + slope * ((lane_x + float(i * N)) - (NX - 1) / 2.0)
            ends = [(NU - 1) / 2.0 + slope * (i * N + end - (NX - 1) / 2.0) for end in (0.0, N - 1.0)]
            tile = jnp.clip(jnp.floor(jnp.minimum(ends[0], ends[1]) * (1.0 / N)), 0.0, float((NU - WIN) // N))
            column = column - tile * float(N)
            weights = jnp.maximum(0.0, 1.0 - jnp.abs(sub - column)).astype(bf16)
            window = rows
            for bit in (8, 4, 2, 1):
                up = tile >= float(bit)
                tile = jnp.where(up, tile - float(bit), tile)
                upper = jnp.broadcast_to(up, (RB, N))
                keep = bit - 1 + WIN // N
                window = [jnp.where(upper, window[k + bit], window[k]) if k + bit < len(window) else window[k] for k in range(keep)]
            g_ref[p * RB : (p + 1) * RB, i * N : (i + 1) * N] = dot(jnp.concatenate(window, axis=1), weights)

    g = g_ref[...]
    g_high = g.astype(bf16)
    g_low = (g - g_high.astype(f32)).astype(bf16)
    loads[5].wait()
    both = dot(jnp.concatenate([g_high, g_low], axis=0), forward_ref[...])
    spectrum = both[:ROWS] + both[ROWS:]
    for half in range(2):
        tall = jnp.concatenate([spectrum[:, k * N : (k + 1) * N] for k in range(4 * half, 4 * half + 4)], axis=0)
        send1[:, 0, half * N : (half + 1) * N] = tall.T
    lane = iota((N, N), 1)
    limits = jnp.where(lane < 64, limit_ref[0, 0], limit_ref[0, 1])
    limit_out[0] = limits[0:1].astype(f32)

    def exchange(src, dst, s):
        for step in STEPS:
            t, dev = place(step)
            pltpu.make_async_remote_copy(src.at[t], dst.at[me], send_sems.at[s], recv_sems.at[s], device_id=dev, device_id_type=MESH).start()
        dst[me] = src[me]

    def arrived(src, dst, s):
        view = dst.at[pl.ds(0, N - 1)]
        pltpu.make_async_copy(view, view, recv_sems.at[s]).wait()

    pl.semaphore_wait(bar, N - 1)
    exchange(send1, recv1, 0)
    for o in range(1, BANDS):
        pltpu.make_async_remote_copy(
            limit_out.at[0], limit_in.at[b], limit_sems.at[0], limit_sems.at[1], device_id=(d, (b + o) & 15), device_id_type=MESH
        ).start()
    limit_in[b] = limit_out[0]

    loads[6].wait()
    detector = iota((RB, NZ), 0).astype(f32)
    tilt = (2.0 * iota((1, NZ), 1).astype(f32) - (NZ - 1)) / (NZ - 1)
    offsets = [0.5 + (HALO - 1) * trig_ref[NANG + angle_ref[p]] * tilt for p in range(NPROJ)]
    away = jnp.concatenate([detector + 16.0 * s - offsets[p] for s in (-1, 0, 1) for p in range(NPROJ)], axis=0)
    for y in range(YB):
        weights = jnp.maximum(0.0, 1.0 - jnp.abs(away - 2.0 * y)).astype(bf16)
        rows_ref[:, y * NZ : (y + 1) * NZ] = dot(weights, small_ref[0]).astype(bf16)
    fy = fold_freq(iota((NY, 1), 0), NY)
    fz = fold_freq(iota((1, NZ), 1), NZ)
    for k in range(KX):
        fx = fold_freq(me * KX + k + iota((1, NZ), 1) * 0, NX)
        radius = fy + (fx + fz)
        low = (radius * (1.0 / (lower_edge * lower_edge))) ** 8
        up = (radius * (1.0 / (upper_edge * upper_edge))) ** 8
        gain_ref[:, k * NZ : (k + 1) * NZ] = low * (math.pi / NPROJ) / ((1.0 + low) * (1.0 + up))

    arrived(send1, recv1, 0)
    group = iota((BANDS, N), 1) >> 5
    field = [[None, None] for _ in range(KX)]
    for half in range(2):
        for j in range(2):
            x = [recv1[(4 * j + q) * BANDS : (4 * j + q + 1) * BANDS, 0, half * N : (half + 1) * N] for q in range(4)]
            for bit in (1, 2):
                clear = (group & bit) == 0
                for q in range(4):
                    if q & bit == 0:
                        a, c = x[q], x[q + bit]
                        x[q] = jnp.where(clear, a, pltpu.roll(c, 32 * bit, 1))
                        x[q + bit] = jnp.where(clear, pltpu.roll(a, N - 32 * bit, 1), c)
            for q in range(4):
                field[4 * half + q][j] = x[q]
    landed = limit_in.at[pl.ds(0, BANDS - 1)]
    pltpu.make_async_copy(landed, landed, limit_sems.at[1]).wait()
    lims = limit_in[:, 0, :]
    swapped = pltpu.roll(lims, 64, 1)
    left = iota((BANDS, N), 1) < 64
    lo, hi = jnp.where(left, lims, swapped), jnp.where(left, swapped, lims)
    columns = []
    for s in (-1, 0, 1):
        row = (16 * (iota((BANDS, N), 0) + s) + (iota((BANDS, N), 1) & 15)).astype(f32)
        ok = (row >= lo) & (row < hi) & (row >= 0.0) & (row < 256.0)
        keep = jnp.where(ok, 1.0, 0.0)
        for j in range(2):
            moved = [field[k][j] if s == 0 else pltpu.roll(field[k][j], (-s) % BANDS, 0) for k in range(KX)]
            columns.append(jnp.concatenate([(m * keep).astype(bf16) for m in moved], axis=0))
    vol = dot(jnp.concatenate(columns, axis=1), rows_ref[...]).astype(bf16)
    tall = [
        jnp.concatenate([vol[k * BANDS : (k + 1) * BANDS, y * NZ : (y + 1) * NZ] for y in range(YB)], axis=0)
        for k in range(KX)
    ]
    along_y = dot(small_ref[1], jnp.concatenate(tall, axis=1))
    back_y = dot(small_ref[2], (along_y * gain_ref[...]).astype(bf16)).astype(bf16)
    for k in range(KX):
        back_ref[:, k * NY : (k + 1) * NY] = lax.dot_general(
            small_ref[0], back_y[:, k * NZ : (k + 1) * NZ], (((1,), (1,)), ((), ())), preferred_element_type=f32
        )
    for chunk in CHUNKS:
        first = pl.multiple_of(place2(chunk[0])[1][0] * BANDS, BANDS)
        for k in range(KX):
            mix_ref[pl.ds(first, BANDS), k, :] = back_ref[pl.ds(first, BANDS), k * NY : (k + 1) * NY]
        send2[pl.ds(first, BANDS)] = mix_ref[pl.ds(first, BANDS)].astype(bf16)
        for step in chunk:
            if any(step):
                t, dev = place2(step)
                pltpu.make_async_remote_copy(send2.at[t], recv2.at[me], send_sems.at[1], recv_sems.at[1], device_id=dev, device_id_type=MESH).start()
    recv2[me] = send2[me]
    arrived(send2, recv2, 1)
    pltpu.make_async_copy(landed, landed, limit_sems.at[0]).wait()
    for s, src in enumerate((send1, send2)):
        view = src.at[pl.ds(0, N - 1)]
        pltpu.make_async_copy(view, view, send_sems.at[s]).wait()


def on_device(projections, angle_index, row_ranges):
    ramp, forward, inverse, small, trig = tables()
    vmem = pl.BlockSpec(memory_space=pltpu.VMEM)
    hbm = pl.BlockSpec(memory_space=pl.ANY)
    back = pl.pallas_call(
        kernel,
        name="laminograph",
        out_shape=jax.ShapeDtypeStruct((N, KX, NY), bf16),
        in_specs=[hbm] * 7,
        out_specs=vmem,
        scratch_shapes=[
            pltpu.SMEM((NPROJ,), jnp.int32),
            pltpu.SMEM((1, 2), jnp.int32),
            pltpu.SMEM(trig.shape, f32),
            pltpu.VMEM((ROWS, NU), bf16),
            pltpu.VMEM(ramp.shape, bf16),
            pltpu.VMEM(forward.shape, bf16),
            pltpu.VMEM(small.shape, bf16),
            pltpu.VMEM((NU // TILE * ROWS, TILE), bf16),
            pltpu.VMEM((ROWS, NU), bf16),
            pltpu.VMEM((ROWS, NX), f32),
            pltpu.VMEM((N, 1, 2 * N), f32),
            pltpu.VMEM((N, 1, 2 * N), f32),
            pltpu.VMEM((3 * 256, YB * NZ), bf16),
            pltpu.VMEM((NZ, KX * NY), f32),
            pltpu.VMEM((NZ, KX * NY), f32),
            pltpu.VMEM((NZ, KX, NY), f32),
            pltpu.VMEM((N, KX, NY), bf16),
            pltpu.VMEM((1, 1, N), f32),
            pltpu.VMEM((BANDS, 1, N), f32),
            pltpu.SemaphoreType.DMA((7,)),
            pltpu.SemaphoreType.DMA((2,)),
            pltpu.SemaphoreType.DMA((2,)),
            pltpu.SemaphoreType.DMA((2,)),
        ],
        compiler_params=pltpu.CompilerParams(collective_id=1, has_side_effects=True, vmem_limit_bytes=24 * 2**20),
    )(*[pltpu.with_memory_space_constraint(x, pltpu.HBM) for x in (angle_index, row_ranges, trig, projections.reshape(ROWS, NU), ramp, forward, small)])
    return lax.dot_general(back.reshape(NX, NY), inverse, (((0,), (0,)), ((), ())), preferred_element_type=f32)[None]


def solution(mesh):
    return jax.shard_map(
        on_device,
        mesh=mesh,
        in_specs=(P("depth", "yband", None), P(), P("yband", None)),
        out_specs=P(("depth", "yband"), None, None),
        check_vma=False,
    )
```

```python
import math

import jax
import jax.numpy as jnp
import numpy as np
from jax import lax
from jax.experimental import pallas as pl
from jax.experimental.pallas import tpu as pltpu
from jax.sharding import PartitionSpec as P

NX, NU, NANG, NY, NZ = 1024, 2048, 1440, 128, 128
NP_DEV, YB, RB, HALO, BANDS, NPROJ = 2, 8, 16, 12, 16, 16
N = 128
KX = NX // N
ROWS = NP_DEV * RB
TILE = 256
WIN = 384
MESH = pl.DeviceIdType.MESH
lower_edge, upper_edge = 0.04, 0.35
f32, bf16 = jnp.float32, jnp.bfloat16


def far_first():
    steps = [(x, y, z, c) for x in range(4) for y in range(4) for z in range(4) for c in range(2)]
    hops = lambda s: sum(min(q, 4 - q) for q in s[:3])
    return sorted(steps, key=lambda s: (-hops(s), s))[:-2] + [(0, 0, 0, 1)]


def far_chunks():
    chunks = []
    for high, y in sorted([(h, y) for h in range(2) for y in range(4)], key=lambda q: (-2 * q[0] - min(q[1], 4 - q[1]), q)):
        inner = [(low, z, c) for low in range(2) for z in range(4) for c in range(2)]
        inner.sort(key=lambda q: (-abs(2 * high - q[0]) - min(q[1], 4 - q[1]), q))
        chunks.append([(high, low, y, z, c) for low, z, c in inner])
    return chunks


STEPS = far_first()
CHUNKS = far_chunks()


def real_basis(n):
    rows = np.arange(n)
    k = np.where(rows <= n // 2, rows, rows - n // 2)
    phase = 2.0 * np.pi * ((k[:, None] * rows[None, :]) % n) / n
    q = np.where((rows <= n // 2)[:, None], np.cos(phase), np.sin(phase))
    norm = np.where((rows == 0) | (rows == n // 2), 1.0 / n, 2.0 / n)
    return q * np.sqrt(norm)[:, None]


def ramp_tiles():
    n = np.arange(-(NU - 1), NU)
    odd = n % 2 != 0
    dist = np.where(odd, n, 1).astype(np.float32)
    values = np.where(n == 0, np.float32(0.25), np.where(odd, np.float32(-1.0) / (np.float32(math.pi * math.pi) * dist * dist), np.float32(0)))
    values = (values / np.float32(NX / NU)).astype(bf16)
    blocks = NU // TILE
    off = np.arange(1 - blocks, blocks)[:, None, None] * TILE
    at = off + np.arange(TILE)[None, :, None] - np.arange(TILE)[None, None, :]
    return values[at + NU - 1]


def tables():
    qx, qy, qz = real_basis(NX), real_basis(NY), real_basis(NZ)
    order = (np.arange(N)[None, :] * KX + np.arange(KX)[:, None]).reshape(-1)
    forward_x = qx.T[:, order]
    by_band = qy.reshape(NY, BANDS, YB).transpose(0, 2, 1).reshape(NY, NY)
    small = np.stack([qz.T, by_band, qy.T])
    angle = (np.float32(2.0 * math.pi) * np.arange(NANG, dtype=np.float32) / np.float32(NANG)).astype(np.float64)
    trig = np.concatenate([np.cos(angle), np.sin(angle)]).astype(np.float32)
    return (
        jnp.asarray(ramp_tiles()),
        jnp.asarray(forward_x.astype(np.float32), bf16),
        jnp.asarray(qx.astype(np.float32), bf16),
        jnp.asarray(small.astype(np.float32), bf16),
        jnp.asarray(trig),
    )


def iota(shape, axis):
    return lax.broadcasted_iota(jnp.int32, shape, axis)


def dot(a, b):
    return jnp.dot(a, b, preferred_element_type=f32)


def fold_freq(row, n):
    k = jnp.where(row <= n // 2, row, row - n // 2).astype(f32) / n
    return k * k


def kernel(
    angle_hbm, limit_hbm, trig_hbm, proj_hbm, ramp_hbm, forward_hbm, small_hbm,
    recv2,
    angle_ref, limit_ref, trig_ref, proj_ref, ramp_ref, forward_ref, small_ref,
    stack_ref, filt_ref, g_ref, send1, recv1, rows_ref, gain_ref, mix_ref, send2,
    limit_out, limit_in, table_sems, send_sems, recv_sems, limit_sems,
):
    d = lax.axis_index("depth")
    b = lax.axis_index("yband")
    me = d * BANDS + b

    px, py = ((d >> 2) << 1) | (b >> 3), d & 3
    pz, pc = (b >> 1) & 3, b & 1

    def place(step):
        dx, dy, dz, dc = step
        x, y, z, c = (px + dx) & 3, (py + dy) & 3, (pz + dz) & 3, pc ^ dc
        dd, bb = ((x >> 1) << 2) | y, ((x & 1) << 3) | (z << 1) | c
        return dd * BANDS + bb, (dd, bb)

    def place2(step):
        high, low, y, z, c = step
        dd = (((d >> 2) ^ high) << 2) | ((py + y) & 3)
        bb = (((b >> 3) ^ low) << 3) | (((pz + z) & 3) << 1) | (pc ^ c)
        return dd * BANDS + bb, (dd, bb)

    pairs = [(proj_hbm, proj_ref), (ramp_hbm, ramp_ref), (angle_hbm, angle_ref), (trig_hbm, trig_ref), (limit_hbm, limit_ref)]
    pairs += [(forward_hbm, forward_ref), (small_hbm, small_ref)]
    loads = [pltpu.make_async_copy(src, dst, table_sems.at[i]) for i, (src, dst) in enumerate(pairs)]
    for i in (0, 1, 5):
        loads[i].start()

    bar = pltpu.get_barrier_semaphore()

    for step in STEPS:
        pl.semaphore_signal(bar, inc=1, device_id=place(step)[1], device_id_type=MESH)

    for i in (2, 3, 4, 6):
        loads[i].start()

    blocks = NU // TILE
    loads[0].wait()
    for i in range(blocks):
        stack_ref[i * ROWS : (i + 1) * ROWS, :] = proj_ref[:, i * TILE : (i + 1) * TILE]
    loads[1].wait()
    acc = [jnp.zeros((ROWS, TILE), f32) for _ in range(blocks)]
    for k in range(1 - blocks, blocks):
        first, last = max(k, 0), blocks + min(k, 0)
        part = dot(stack_ref[first * ROWS : last * ROWS, :], ramp_ref[k + blocks - 1])
        for i in range(first, last):
            acc[i - k] += part[(i - first) * ROWS : (i - first + 1) * ROWS]
    for j in range(blocks):
        filt_ref[:, j * TILE : (j + 1) * TILE] = acc[j].astype(bf16)

    for load in loads[2:5]:
        load.wait()
    sub = iota((WIN, N), 0).astype(f32)
    lane_x = iota((1, N), 1).astype(f32)
    for p in range(NP_DEV):
        slope = jnp.full((1, N), 2.0 * trig_ref[angle_ref[d * NP_DEV + p]])
        rows = [filt_ref[p * RB : (p + 1) * RB, i * N : (i + 1) * N] for i in range(NU // N)]
        for i in range(NX // N):
            column = (NU - 1) / 2.0 + slope * ((lane_x + float(i * N)) - (NX - 1) / 2.0)
            ends = [(NU - 1) / 2.0 + slope * (i * N + end - (NX - 1) / 2.0) for end in (0.0, N - 1.0)]
            tile = jnp.clip(jnp.floor(jnp.minimum(ends[0], ends[1]) * (1.0 / N)), 0.0, float((NU - WIN) // N))
            column = column - tile * float(N)
            weights = jnp.maximum(0.0, 1.0 - jnp.abs(sub - column)).astype(bf16)
            window = rows
            for bit in (8, 4, 2, 1):
                up = tile >= float(bit)
                tile = jnp.where(up, tile - float(bit), tile)
                upper = jnp.broadcast_to(up, (RB, N))
                keep = bit - 1 + WIN // N
                window = [jnp.where(upper, window[k + bit], window[k]) if k + bit < len(window) else window[k] for k in range(keep)]
            g_ref[p * RB : (p + 1) * RB, i * N : (i + 1) * N] = dot(jnp.concatenate(window, axis=1), weights)

    g = g_ref[...]
    g_high = g.astype(bf16)
    g_low = (g - g_high.astype(f32)).astype(bf16)
    loads[5].wait()
    both = dot(jnp.concatenate([g_high, g_low], axis=0), forward_ref[...])
    spectrum = both[:ROWS] + both[ROWS:]
    for half in range(2):
        tall = jnp.concatenate([spectrum[:, k * N : (k + 1) * N] for k in range(4 * half, 4 * half + 4)], axis=0)
        send1[:, 0, half * N : (half + 1) * N] = tall.T
    lane = iota((N, N), 1)
    limits = jnp.where(lane < 64, limit_ref[0, 0], limit_ref[0, 1])
    limit_out[0] = limits[0:1].astype(f32)

    def exchange(src, dst, s):
        for step in STEPS:
            t, dev = place(step)
            pltpu.make_async_remote_copy(src.at[t], dst.at[me], send_sems.at[s], recv_sems.at[s], device_id=dev, device_id_type=MESH).start()
        dst[me] = src[me]

    def arrived(src, dst, s):
        view = dst.at[pl.ds(0, N - 1)]
        pltpu.make_async_copy(view, view, recv_sems.at[s]).wait()

    pl.semaphore_wait(bar, N - 1)
    exchange(send1, recv1, 0)
    for o in range(1, BANDS):
        pltpu.make_async_remote_copy(
            limit_out.at[0], limit_in.at[b], limit_sems.at[0], limit_sems.at[1], device_id=(d, (b + o) & 15), device_id_type=MESH
        ).start()
    limit_in[b] = limit_out[0]

    loads[6].wait()
    detector = iota((RB, NZ), 0).astype(f32)
    tilt = (2.0 * iota((1, NZ), 1).astype(f32) - (NZ - 1)) / (NZ - 1)
    offsets = [0.5 + (HALO - 1) * trig_ref[NANG + angle_ref[p]] * tilt for p in range(NPROJ)]
    away = jnp.concatenate([detector + 16.0 * s - offsets[p] for s in (-1, 0, 1) for p in range(NPROJ)], axis=0)
    for y in range(YB):
        weights = jnp.maximum(0.0, 1.0 - jnp.abs(away - 2.0 * y)).astype(bf16)
        rows_ref[:, y * NZ : (y + 1) * NZ] = dot(weights, small_ref[0]).astype(bf16)
    fy = fold_freq(iota((NY, 1), 0), NY)
    fz = fold_freq(iota((1, NZ), 1), NZ)
    for k in range(KX):
        fx = fold_freq(me * KX + k + iota((1, NZ), 1) * 0, NX)
        radius = fy + (fx + fz)
        low = (radius * (1.0 / (lower_edge * lower_edge))) ** 8
        up = (radius * (1.0 / (upper_edge * upper_edge))) ** 8
        gain_ref[:, k * NZ : (k + 1) * NZ] = low * (math.pi / NPROJ) / ((1.0 + low) * (1.0 + up))

    arrived(send1, recv1, 0)
    group = iota((BANDS, N), 1) >> 5
    field = [[None, None] for _ in range(KX)]
    for half in range(2):
        for j in range(2):
            x = [recv1[(4 * j + q) * BANDS : (4 * j + q + 1) * BANDS, 0, half * N : (half + 1) * N] for q in range(4)]
            for bit in (1, 2):
                clear = (group & bit) == 0
                for q in range(4):
                    if q & bit == 0:
                        a, c = x[q], x[q + bit]
                        x[q] = jnp.where(clear, a, pltpu.roll(c, 32 * bit, 1))
                        x[q + bit] = jnp.where(clear, pltpu.roll(a, N - 32 * bit, 1), c)
            for q in range(4):
                field[4 * half + q][j] = x[q]
    landed = limit_in.at[pl.ds(0, BANDS - 1)]
    pltpu.make_async_copy(landed, landed, limit_sems.at[1]).wait()
    lims = limit_in[:, 0, :]
    swapped = pltpu.roll(lims, 64, 1)
    left = iota((BANDS, N), 1) < 64
    lo, hi = jnp.where(left, lims, swapped), jnp.where(left, swapped, lims)
    columns = []
    for s in (-1, 0, 1):
        row = (16 * (iota((BANDS, N), 0) + s) + (iota((BANDS, N), 1) & 15)).astype(f32)
        ok = (row >= lo) & (row < hi) & (row >= 0.0) & (row < 256.0)
        keep = jnp.where(ok, 1.0, 0.0)
        for j in range(2):
            moved = [field[k][j] if s == 0 else pltpu.roll(field[k][j], (-s) % BANDS, 0) for k in range(KX)]
            columns.append(jnp.concatenate([(m * keep).astype(bf16) for m in moved], axis=0))
    vol = dot(jnp.concatenate(columns, axis=1), rows_ref[...]).astype(bf16)
    tall = [
        jnp.concatenate([vol[k * BANDS : (k + 1) * BANDS, y * NZ : (y + 1) * NZ] for y in range(YB)], axis=0)
        for k in range(KX)
    ]
    along_y = dot(small_ref[1], jnp.concatenate(tall, axis=1))
    back_y = dot(small_ref[2], (along_y * gain_ref[...]).astype(bf16)).astype(bf16)
    for k in range(KX):
        mix_ref[:, k, :] = lax.dot_general(
            small_ref[0], back_y[:, k * NZ : (k + 1) * NZ], (((1,), (1,)), ((), ())), preferred_element_type=f32
        )
    for chunk in CHUNKS:
        first = pl.multiple_of(place2(chunk[0])[1][0] * BANDS, BANDS)
        send2[pl.ds(first, BANDS)] = mix_ref[pl.ds(first, BANDS)].astype(bf16)
        for step in chunk:
            if any(step):
                t, dev = place2(step)
                pltpu.make_async_remote_copy(send2.at[t], recv2.at[me], send_sems.at[1], recv_sems.at[1], device_id=dev, device_id_type=MESH).start()
    recv2[me] = send2[me]
    arrived(send2, recv2, 1)
    pltpu.make_async_copy(landed, landed, limit_sems.at[0]).wait()
    for s, src in enumerate((send1, send2)):
        view = src.at[pl.ds(0, N - 1)]
        pltpu.make_async_copy(view, view, send_sems.at[s]).wait()


def on_device(projections, angle_index, row_ranges):
    ramp, forward, inverse, small, trig = tables()
    vmem = pl.BlockSpec(memory_space=pltpu.VMEM)
    hbm = pl.BlockSpec(memory_space=pl.ANY)
    back = pl.pallas_call(
        kernel,
        name="laminograph",
        out_shape=jax.ShapeDtypeStruct((N, KX, NY), bf16),
        in_specs=[hbm] * 7,
        out_specs=vmem,
        scratch_shapes=[
            pltpu.SMEM((NPROJ,), jnp.int32),
            pltpu.SMEM((1, 2), jnp.int32),
            pltpu.SMEM(trig.shape, f32),
            pltpu.VMEM((ROWS, NU), bf16),
            pltpu.VMEM(ramp.shape, bf16),
            pltpu.VMEM(forward.shape, bf16),
            pltpu.VMEM(small.shape, bf16),
            pltpu.VMEM((NU // TILE * ROWS, TILE), bf16),
            pltpu.VMEM((ROWS, NU), bf16),
            pltpu.VMEM((ROWS, NX), f32),
            pltpu.VMEM((N, 1, 2 * N), f32),
            pltpu.VMEM((N, 1, 2 * N), f32),
            pltpu.VMEM((3 * 256, YB * NZ), bf16),
            pltpu.VMEM((NZ, KX * NY), f32),
            pltpu.VMEM((NZ, KX, NY), f32),
            pltpu.VMEM((N, KX, NY), bf16),
            pltpu.VMEM((1, 1, N), f32),
            pltpu.VMEM((BANDS, 1, N), f32),
            pltpu.SemaphoreType.DMA((7,)),
            pltpu.SemaphoreType.DMA((2,)),
            pltpu.SemaphoreType.DMA((2,)),
            pltpu.SemaphoreType.DMA((2,)),
        ],
        compiler_params=pltpu.CompilerParams(collective_id=1, has_side_effects=True, vmem_limit_bytes=24 * 2**20),
    )(*[pltpu.with_memory_space_constraint(x, pltpu.HBM) for x in (angle_index, row_ranges, trig, projections.reshape(ROWS, NU), ramp, forward, small)])
    return lax.dot_general(back.reshape(NX, NY), inverse, (((0,), (0,)), ((), ())), preferred_element_type=f32)[None]


def solution(mesh):
    return jax.shard_map(
        on_device,
        mesh=mesh,
        in_specs=(P("depth", "yband", None), P(), P("yband", None)),
        out_specs=P(("depth", "yband"), None, None),
        check_vma=False,
    )
```
